32 devices in a mesh: terms: 8 (over y, x, core), sectors: 4 (over z).
Axes of the slice: x: 2, y: 2, z: 4, core: 2. Of those that a mesh axis runs over, the one named last changes fastest.
Arguments:
- trial: float32 [4, 128, 128], P('sectors'), may hold values from -6 to 6
- precond: float32 [4, 128, 128], P('sectors'), may hold values from 1 to 8
- block_rows: int32 [4], replicated, may hold values from 64 to 128
- owner_map: int32 [4], replicated, may hold values from 0 to 3, each once
- term_in: int32 [2048], P(('terms', 'sectors')), may hold values from 0 to 3
- term_out: int32 [2048], P(('terms', 'sectors')), may hold values from 0 to 3
- left_ops: bfloat16 [2048, 128, 128], P(('terms', 'sectors')), may hold values from -0.15462404 to 1.16462404
- right_ops: bfloat16 [2048, 128, 128], P(('terms', 'sectors')), may hold values from -0.0068334817 to 0.010778794
Outputs:
- vector: float32 [4, 128, 128], P('sectors')
- energies: float32 [3], replicated
The draws below stay inside these ranges and needn't reach their ends.
All inputs are finite; a program needn't handle non-finite values.
Results may differ from the reference program's by a relative error of at most 0.0036.
Values may be sent and summed in bfloat16 or wider, within the bound.
No kernel may reach another device: no remote copies, remote signals or barrier semaphores. Data moves between devices by JAX's collectives and lax.ppermute only.
A program may use at most 64 MiB of HBM per device.

```python
import math
import jax
import jax.numpy as jnp
import numpy as np
from jax import lax

ROWS = 128
COLS = 128
K_DEV = 64
STEPS = 3
SECTORS = 4
TERMS = 2048


def draw_left_ops(key, part):
    key = jax.random.fold_in(key, 11)
    half_width = 1.7320508 * ROWS ** (-0.5)
    noise = jax.random.uniform(key, (TERMS, ROWS, ROWS), jnp.float32, -half_width, half_width)
    diagonal_part = jnp.eye(ROWS, dtype=jnp.float32)
    return (noise + diagonal_part[None, :, :]).astype(jnp.bfloat16)


def draw_right_ops(key, part):
    key = jax.random.fold_in(key, 23)
    half_width = 1.7320508 * (COLS * TERMS / SECTORS) ** (-0.5)
    bias_level = SECTORS ** 1.5 / TERMS
    noise = jax.random.uniform(key, (TERMS, COLS, COLS), jnp.float32, -half_width, half_width)
    diagonal_part = bias_level * jnp.eye(COLS, dtype=jnp.float32)
    return (noise + diagonal_part[None, :, :]).astype(jnp.bfloat16)


def with_ends(drawn, key, low, top_value):
    extent = drawn.shape
    index_at = [jax.random.randint(jax.random.fold_in(key, axis), (), 0, extent[axis]) for axis in range(len(extent))]
    drawn = drawn.at[tuple(index_at)].set(low)
    longest = extent.index(max(extent))
    index_at[longest] = (index_at[longest] + 1) % extent[longest]
    return drawn.at[tuple(index_at)].set(top_value)


def block_scale(key, shape, cuts, smallest, top_value):
    gain = 1.0
    for position, parts in cuts:
        draws = jax.random.uniform(jax.random.fold_in(jax.random.fold_in(key, 6), position), (parts,), jnp.float32, smallest / len(cuts), top_value / len(cuts))
        gain = gain * jnp.repeat(jnp.exp(draws), shape[position] // parts).reshape((-1,) + (1,) * (len(shape) - 1 - position))
    return gain


def rank_bounds(count, lean):
    loads = [(1 << 20) // math.isqrt(standing ** lean) + 1 for standing in range(1, count + 1)]
    scale = 1 + sum(loads) // (1 << 30)
    return np.cumsum(np.array([max(1, weight // scale) for weight in loads]))


def ranked_ids(rng, extent, amount, lean):
    grid = rank_bounds(amount, lean)
    ticket = jax.random.randint(jax.random.fold_in(rng, 1), extent, 0, int(grid[amount - 1]))
    rank = jnp.searchsorted(jnp.asarray(grid, jnp.int32), ticket, side="right")
    return jax.random.permutation(jax.random.fold_in(rng, 2), amount)[rank].astype(jnp.int32)


def centred(rng, shape, deviation, bound, pieces=(), kind=jnp.bfloat16):
    loudness = block_scale(rng, shape, pieces, -0.22, 0.18) if pieces else 1.0
    array = jax.random.normal(rng, shape, jnp.float32) * deviation * loudness
    return jnp.minimum(jnp.maximum(array, -bound), bound).astype(kind)


def setup_inputs(seed: int = 0) -> dict:
    keys = jax.random.split(jax.random.key(seed), 9)
    trial = centred(keys[0], (SECTORS, ROWS, COLS), 1.0, 6.0, ((0, 4),), jnp.float32)
    precond = jnp.clip(jnp.exp(math.log(8.0) - 2.0794415 * jax.random.uniform(keys[1], (SECTORS, ROWS, COLS), jnp.float32) ** block_scale(keys[1], (SECTORS, ROWS, COLS), ((0, 4),), -0.2, 0.2)), 1.0, 8.0)
    block_rows = with_ends(jax.random.randint(keys[2], (SECTORS,), ROWS // 2, ROWS + 1), jax.random.fold_in(keys[2], 1), ROWS // 2, ROWS).astype(jnp.int32)
    owner_map = jax.random.permutation(keys[3], SECTORS).astype(jnp.int32)
    term_in = with_ends(jax.random.randint(keys[4], (TERMS,), 0, SECTORS), jax.random.fold_in(keys[4], 1), 0, SECTORS - 1).astype(jnp.int32)
    term_out = with_ends(ranked_ids(keys[5], (TERMS,), SECTORS, 2), jax.random.fold_in(keys[5], 3), 0, SECTORS - 1).astype(jnp.int32)
    left_ops = draw_left_ops(jax.random.fold_in(keys[8], 71), 0)
    right_ops = draw_right_ops(jax.random.fold_in(keys[8], 71), 0)
    return {"trial": trial, "precond": precond, "block_rows": block_rows, "owner_map": owner_map, "term_in": term_in, "term_out": term_out, "left_ops": left_ops, "right_ops": right_ops}


def live_mask(block_rows):
    rows_index = jnp.arange(ROWS, dtype=jnp.int32)
    return (rows_index[None, :] < block_rows[:, None]).astype(jnp.float32)[:, :, None]

def reference(trial, precond, block_rows, owner_map, term_in, term_out, left_ops, right_ops):
    slot_of = jnp.zeros((SECTORS,), jnp.int32).at[owner_map].set(jnp.arange(SECTORS, dtype=jnp.int32))
    in_slot = slot_of[term_in].astype(jnp.int32)
    out_slot = slot_of[term_out].astype(jnp.int32)
    masking = live_mask(block_rows)
    vector = trial * masking
    entry_count = float(SECTORS * ROWS * COLS)
    groups = (left_ops.reshape(-1, K_DEV, ROWS, ROWS), right_ops.reshape(-1, K_DEV, COLS, COLS), in_slot.reshape(-1, K_DEV), out_slot.reshape(-1, K_DEV))
    energies = []
    for iteration in range(STEPS):
        blocks = vector.astype(jnp.bfloat16)

        def accumulate(sigma, group):
            left_group, right_group, source, target = group
            picked = blocks[source].astype(jnp.float32)
            halves = jnp.einsum('kab,kbc->kac', left_group.astype(jnp.float32), picked, precision=lax.Precision.HIGHEST).astype(jnp.bfloat16)
            contrib = jnp.einsum('kac,kcd->kad', halves.astype(jnp.float32), right_group.astype(jnp.float32), precision=lax.Precision.HIGHEST)
            return (sigma.at[target].add(contrib), None)
        sigma, unused = lax.scan(accumulate, jnp.zeros((SECTORS, ROWS, COLS), jnp.float32), groups)
        sigma = sigma * masking - precond * vector
        rayleigh = jnp.sum(vector * sigma) / jnp.sum(vector * vector)
        updated = vector - (sigma - rayleigh * vector) / precond
        vector = updated / jnp.sqrt(jnp.sum(updated * updated) / entry_count + 1e-06)
        energies.append(rayleigh)
    return (vector, jnp.stack(energies))
```

```python
import functools
import math

import jax
import jax.numpy as jnp
from jax import lax
from jax.experimental import pallas as pl
from jax.experimental.pallas import tpu as pltpu
from jax.sharding import PartitionSpec as P

STEPS = 3
UNROLL = 16
LEFT_MAX = 1.16462404
RIGHT_MAX = 0.010778794
VMEM = pl.BlockSpec(memory_space=pltpu.VMEM)
SMEM = pl.BlockSpec(memory_space=pltpu.SMEM)
F32 = jnp.float32
BF16 = jnp.bfloat16
HALF = jnp.float16


def total(tile):
    return jnp.sum(jnp.sum(tile, axis=0, keepdims=True), axis=1, keepdims=True)


def lanes(x):
    rows, cols = x.shape
    return jnp.sum(x.reshape(rows // 8, 8, cols), axis=0)


def live(rows_ref, g, shape):
    return lax.broadcasted_iota(jnp.int32, shape, 0) < rows_ref[g]


def apply_ops(wire, square, blocks, slot, acc, refs, keep, send):
    owner, term_in, term_out, left, right = refs
    sectors, rows, cols = acc.shape
    for i in range(sectors):
        slot[owner[i]] = i
    acc[...] = jnp.zeros_like(acc)
    terms = left.shape[0]
    unroll = math.gcd(UNROLL, terms)

    def group(j, carry):
        for u in range(unroll):
            k = j * unroll + u
            half = jnp.dot(left[k], blocks[slot[term_in[k]]], preferred_element_type=F32)
            acc[slot[term_out[k]]] += jnp.dot(half.astype(BF16), right[k], preferred_element_type=F32)
        return carry

    lax.fori_loop(0, terms // unroll, group, 0)
    gain = (wire / jnp.sqrt(square / (sectors * rows * cols)))[None]
    h = sectors // 2
    low = lax.axis_index("terms") % 2
    keep[...] = acc[pl.ds(low * h, h)] * gain
    send[...] = acc[pl.ds((1 - low) * h, h)] * gain


def first_kernel(wire, mine, other, rows_live, owner, term_in, term_out, left, right,
                 vec, pre, state, keep, send, blocks, slot, acc):
    sectors, rows, cols = acc.shape
    low = lax.axis_index("terms") % 2

    def load(trial, precond):
        for g in range(sectors):
            vec[g] = jnp.where(live(rows_live, g, (rows, cols)), trial[g], 0.0)
            pre[g] = precond[g]

    @pl.when(low == 0)
    def _():
        load(mine, other)

    @pl.when(low == 1)
    def _():
        load(other, mine)

    tile = jnp.zeros((8, cols), F32)
    for g in range(sectors):
        v = vec[g]
        blocks[g] = v.astype(BF16)
        tile = tile + lanes(v * v)
    square = jnp.maximum(total(tile), 1e-30)
    state[...] = jnp.broadcast_to(square, state.shape)
    apply_ops(wire, square, blocks, slot, acc, (owner, term_in, term_out, left, right), keep, send)


def update(wire, own, far, rows_live, vec, pre, square, full, out):
    sectors, rows, cols = full.shape
    h = sectors // 2
    low = lax.axis_index("terms") % 2
    full[pl.ds(low * h, h)] = own[...]
    full[pl.ds((1 - low) * h, h)] = far[...]
    gain = jnp.sqrt(square / (sectors * rows * cols)) / wire
    tile = jnp.zeros((8, cols), F32)
    for g in range(sectors):
        v = vec[g]
        summed = jnp.where(live(rows_live, g, (rows, cols)), full[g] * gain, 0.0)
        full[g] = summed
        tile = tile + lanes(v * (summed - pre[g] * v))
    rayleigh = total(tile) / square
    tile = jnp.zeros((8, cols), F32)
    for g in range(sectors):
        v = vec[g]
        u = 2.0 * v - (full[g] - rayleigh * v) / pre[g]
        out[g] = u
        tile = tile + lanes(u * u)
    scale = 1.0 / jnp.sqrt(total(tile) / (sectors * rows * cols) + 1e-06)
    return rayleigh, scale


def middle_kernel(wire, step, own, far, vec_in, pre, state_in, rows_live, owner, term_in, term_out, left, right,
                  vec, state, keep, send, full, blocks, slot, acc):
    sectors, rows, cols = acc.shape
    old = state_in[...]
    rayleigh, scale = update(wire, own, far, rows_live, vec_in, pre, old[0:1, 0:1], full, vec)
    tile = jnp.zeros((8, cols), F32)
    for g in range(sectors):
        v = vec[g] * scale
        vec[g] = v
        blocks[g] = v.astype(BF16)
        tile = tile + lanes(v * v)
    square = jnp.maximum(total(tile), 1e-30)
    line = lax.broadcasted_iota(jnp.int32, old.shape, 0)
    state[...] = jnp.where(line == 0, square, jnp.where(line == step, rayleigh, old))
    apply_ops(wire, square, blocks, slot, acc, (owner, term_in, term_out, left, right), keep, send)


def last_kernel(wire, step, own, far, vec_in, pre, state_in, rows_live, out, energies, full, fresh):
    held = out.shape[0]
    old = state_in[...]
    rayleigh, scale = update(wire, own, far, rows_live, vec_in, pre, old[0:1, 0:1], full, fresh)
    first = lax.axis_index("sectors") * held
    out[...] = fresh[pl.ds(first, held)] * scale[None]
    line = lax.broadcasted_iota(jnp.int32, old.shape, 0)
    energies[...] = jnp.where(line == step, rayleigh, old)


def place_kernel(axis, low_bits, bits, *refs):
    parts, out = refs[:-1], refs[-1]
    size = parts[0].shape[0]
    at = (lax.axis_index(axis) >> low_bits) & ((1 << bits) - 1)
    for mask, part in enumerate(parts):
        out[pl.ds((at ^ mask) * size, size)] = part[...]


def params():
    return pltpu.CompilerParams(vmem_limit_bytes=24 << 20)


def swap(x, axis, mask):
    return lax.ppermute(x, axis, [(i, i ^ mask) for i in range(lax.axis_size(axis))])


def bit_groups(axis, first):
    count = lax.axis_size(axis).bit_length() - 1
    return [(low, min(2, count - low)) for low in range(first, count, 2)]


def sum_stage(x, axis, low, bits):
    got = [x] + [swap(x, axis, mask << low) for mask in range(1, 1 << bits)]
    got = [g.astype(F32) for g in got]
    while len(got) > 1:
        got = [got[i] + got[i + 1] for i in range(0, len(got), 2)]
    return got[0]


def reduce_half(keep, send):
    x = keep + swap(send, "terms", 1)
    for axis, first in (("sectors", 0), ("terms", 1)):
        for low, bits in bit_groups(axis, first):
            x = sum_stage(lax.optimization_barrier(x.astype(HALF)), axis, low, bits)
    return x


def gather(x):
    for low, bits in bit_groups("sectors", 0):
        parts = [x] + [swap(x, "sectors", mask << low) for mask in range(1, 1 << bits)]
        x = pl.pallas_call(
            functools.partial(place_kernel, "sectors", low, bits),
            out_shape=jax.ShapeDtypeStruct((x.shape[0] << bits, *x.shape[1:]), x.dtype),
            in_specs=[VMEM] * len(parts),
            out_specs=VMEM,
        )(*parts)
    return x


def on_device(trial, precond, block_rows, owner_map, term_in, term_out, left_ops, right_ops):
    sec_local, rows, cols = trial.shape
    sectors = sec_local * lax.axis_size("sectors")
    terms = left_ops.shape[0] * lax.axis_size("sectors") * lax.axis_size("terms")
    bound = 1.02 * LEFT_MAX * RIGHT_MAX * math.sqrt(rows * cols) * math.sqrt(sectors * rows * cols) * terms
    wire = 2.0 ** -max(0, math.ceil(math.log2(bound / 65504.0)))
    whole = jax.ShapeDtypeStruct((sectors, rows, cols), F32)
    part = jax.ShapeDtypeStruct((sectors // 2, rows, cols), F32)
    state_shape = jax.ShapeDtypeStruct((8, cols), F32)
    full = pltpu.VMEM((sectors, rows, cols), F32)
    scratch = [pltpu.VMEM((sectors, rows, cols), BF16), pltpu.SMEM((sectors,), jnp.int32), full]
    ints = (block_rows, owner_map, term_in, term_out)

    mine = gather(jnp.where(lax.axis_index("terms") % 2 == 0, trial, precond))
    other = swap(mine, "terms", 1)
    vec, pre, state, keep, send = pl.pallas_call(
        functools.partial(first_kernel, wire),
        out_shape=(whole, whole, state_shape, part, part),
        in_specs=[VMEM] * 2 + [SMEM] * 4 + [VMEM] * 2,
        out_specs=(VMEM,) * 5,
        scratch_shapes=scratch,
        compiler_params=params(),
    )(mine, other, *ints, left_ops, right_ops)
    for step in range(1, STEPS):
        own = reduce_half(keep, send)
        far = swap(own, "terms", 1)
        vec, state, keep, send = pl.pallas_call(
            functools.partial(middle_kernel, wire, step),
            out_shape=(whole, state_shape, part, part),
            in_specs=[VMEM] * 5 + [SMEM] * 4 + [VMEM] * 2,
            out_specs=(VMEM,) * 4,
            scratch_shapes=[full] + scratch,
            compiler_params=params(),
        )(own, far, vec, pre, state, *ints, left_ops, right_ops)
    own = reduce_half(keep, send)
    far = swap(own, "terms", 1)
    vector, energies = pl.pallas_call(
        functools.partial(last_kernel, wire, STEPS),
        out_shape=(jax.ShapeDtypeStruct(trial.shape, F32), state_shape),
        in_specs=[VMEM] * 5 + [SMEM],
        out_specs=(VMEM,) * 2,
        scratch_shapes=[full, full],
        compiler_params=params(),
    )(own, far, vec, pre, state, block_rows)
    return vector, energies[1 : STEPS + 1, 0]


def solution(mesh):
    return jax.shard_map(
        on_device,
        mesh=mesh,
        in_specs=(
            P("sectors", None, None),
            P("sectors", None, None),
            P(),
            P(),
            P(("terms", "sectors")),
            P(("terms", "sectors")),
            P(("terms", "sectors"), None, None),
            P(("terms", "sectors"), None, None),
        ),
        out_specs=(P("sectors", None, None), P()),
        check_vma=False,
    )
```

```python
import functools
import math

import jax
import jax.numpy as jnp
from jax import lax
from jax.experimental import pallas as pl
from jax.experimental.pallas import tpu as pltpu
from jax.sharding import PartitionSpec as P

STEPS = 3
UNROLL = 16
LEFT_MAX = 1.16462404
RIGHT_MAX = 0.010778794
VMEM = pl.BlockSpec(memory_space=pltpu.VMEM)
HBM = pl.BlockSpec(memory_space=pltpu.HBM)
SMEM = pl.BlockSpec(memory_space=pltpu.SMEM)
F32 = jnp.float32
BF16 = jnp.bfloat16
HALF = jnp.float16


def total(tile):
    return jnp.sum(jnp.sum(tile, axis=0, keepdims=True), axis=1, keepdims=True)


def lanes(x):
    rows, cols = x.shape
    return jnp.sum(x.reshape(rows // 8, 8, cols), axis=0)


def live(table, g, acc):
    sectors, rows, cols = acc.shape
    return lax.broadcasted_iota(jnp.int32, (rows, cols), 0) < table[table.shape[0] - sectors + g]


def apply_ops(wire, square, blocks, acc, table, left, right, keep, send):
    sectors, rows, cols = acc.shape
    acc[...] = jnp.zeros_like(acc)
    terms = left.shape[0]
    unroll = math.gcd(UNROLL, terms)

    def group(j, carry):
        for u in range(unroll):
            k = j * unroll + u
            half = jnp.dot(left[k], blocks[table[k]], preferred_element_type=F32)
            acc[table[terms + k]] += jnp.dot(half.astype(BF16), right[k], preferred_element_type=F32)
        return carry

    lax.fori_loop(0, terms // unroll, group, 0)
    gain = (wire / jnp.sqrt(square / (sectors * rows * cols)))[None]
    h = sectors // 2
    low = lax.axis_index("terms") % 2
    keep[...] = acc[pl.ds(low * h, h)] * gain
    send[...] = acc[pl.ds((1 - low) * h, h)] * gain


def load_kernel(rows_hbm, owner_hbm, in_hbm, out_hbm, left_hbm, right_hbm, left, right, table,
                rows_live, owner, term_in, term_out, slot, sems):
    pairs = ((owner_hbm, owner), (in_hbm, term_in), (out_hbm, term_out), (rows_hbm, rows_live),
             (left_hbm, left), (right_hbm, right))
    copies = [pltpu.make_async_copy(src, dst, sems.at[i]) for i, (src, dst) in enumerate(pairs)]
    for copy in copies:
        copy.start()
    for copy in copies[:4]:
        copy.wait()
    sectors, terms = owner.shape[0], term_in.shape[0]
    for i in range(sectors):
        slot[owner[i]] = i
        table[2 * terms + i] = rows_live[i]
    for k in range(terms):
        table[k] = slot[term_in[k]]
        table[terms + k] = slot[term_out[k]]
    for copy in copies[4:]:
        copy.wait()


def first_kernel(wire, *refs):
    table, left, right, vec, pre, state, keep, send, blocks, acc = refs[-10:]
    sectors, rows, cols = acc.shape
    parts = (len(refs) - 10) // 2
    mine, other = refs[:parts], refs[parts : 2 * parts]
    held = sectors // parts
    low = lax.axis_index("terms") % 2
    here = lax.axis_index("sectors")

    def load(trial, precond):
        for mask in range(parts):
            for i in range(held):
                g = (here ^ mask) * held + i
                vec[g] = jnp.where(live(table, g, acc), trial[mask][i], 0.0)
                pre[g] = precond[mask][i]

    @pl.when(low == 0)
    def _():
        load(mine, other)

    @pl.when(low == 1)
    def _():
        load(other, mine)

    tile = jnp.zeros((8, cols), F32)
    for g in range(sectors):
        v = vec[g]
        blocks[g] = v.astype(BF16)
        tile = tile + lanes(v * v)
    square = jnp.maximum(total(tile), 1e-30)
    state[...] = jnp.broadcast_to(square, state.shape)
    apply_ops(wire, square, blocks, acc, table, left, right, keep, send)


def update(wire, own, far, table, vec, pre, square, full, out):
    sectors, rows, cols = full.shape
    h = sectors // 2
    low = lax.axis_index("terms") % 2
    full[pl.ds(low * h, h)] = own[...]
    full[pl.ds((1 - low) * h, h)] = far[...]
    gain = jnp.sqrt(square / (sectors * rows * cols)) / wire
    tile = jnp.zeros((8, cols), F32)
    for g in range(sectors):
        v = vec[g]
        summed = jnp.where(live(table, g, full), full[g] * gain, 0.0)
        full[g] = summed
        tile = tile + lanes(v * (summed - pre[g] * v))
    rayleigh = total(tile) / square
    tile = jnp.zeros((8, cols), F32)
    for g in range(sectors):
        v = vec[g]
        u = 2.0 * v - (full[g] - rayleigh * v) / pre[g]
        out[g] = u
        tile = tile + lanes(u * u)
    scale = 1.0 / jnp.sqrt(total(tile) / (sectors * rows * cols) + 1e-06)
    return rayleigh, scale


def middle_kernel(wire, step, own, far, vec_in, pre, state_in, table, left, right,
                  vec, state, keep, send, full, blocks, acc):
    sectors, rows, cols = acc.shape
    old = state_in[...]
    rayleigh, scale = update(wire, own, far, table, vec_in, pre, old[0:1, 0:1], full, vec)
    tile = jnp.zeros((8, cols), F32)
    for g in range(sectors):
        v = vec[g] * scale
        vec[g] = v
        blocks[g] = v.astype(BF16)
        tile = tile + lanes(v * v)
    square = jnp.maximum(total(tile), 1e-30)
    line = lax.broadcasted_iota(jnp.int32, old.shape, 0)
    state[...] = jnp.where(line == 0, square, jnp.where(line == step, rayleigh, old))
    apply_ops(wire, square, blocks, acc, table, left, right, keep, send)


def last_kernel(wire, step, own, far, vec_in, pre, state_in, table, out, energies, full, fresh):
    held = out.shape[0]
    old = state_in[...]
    rayleigh, scale = update(wire, own, far, table, vec_in, pre, old[0:1, 0:1], full, fresh)
    first = lax.axis_index("sectors") * held
    out[...] = fresh[pl.ds(first, held)] * scale[None]
    line = lax.broadcasted_iota(jnp.int32, old.shape, 0)
    energies[...] = jnp.where(line == step, rayleigh, old)


def params():
    return pltpu.CompilerParams(vmem_limit_bytes=24 << 20)


def swap(x, axis, mask):
    return lax.ppermute(x, axis, [(i, i ^ mask) for i in range(lax.axis_size(axis))])


def bit_groups(axis, first):
    count = lax.axis_size(axis).bit_length() - 1
    return [(low, min(2, count - low)) for low in range(first, count, 2)]


def sum_stage(x, axis, low, bits):
    got = [x] + [swap(x, axis, mask << low) for mask in range(1, 1 << bits)]
    got = [g.astype(F32) for g in got]
    while len(got) > 1:
        got = [got[i] + got[i + 1] for i in range(0, len(got), 2)]
    return got[0]


def reduce_half(keep, send):
    x = keep + swap(send, "terms", 1)
    for axis, first in (("sectors", 0), ("terms", 1)):
        for low, bits in bit_groups(axis, first):
            x = sum_stage(lax.optimization_barrier(x.astype(HALF)), axis, low, bits)
    return x


def on_device(trial, precond, block_rows, owner_map, term_in, term_out, left_ops, right_ops):
    sec_local, rows, cols = trial.shape
    sectors = sec_local * lax.axis_size("sectors")
    terms = left_ops.shape[0] * lax.axis_size("sectors") * lax.axis_size("terms")
    bound = 1.02 * LEFT_MAX * RIGHT_MAX * math.sqrt(rows * cols) * math.sqrt(sectors * rows * cols) * terms
    wire = 2.0 ** -max(0, math.ceil(math.log2(bound / 65504.0)))
    whole = jax.ShapeDtypeStruct((sectors, rows, cols), F32)
    part = jax.ShapeDtypeStruct((sectors // 2, rows, cols), F32)
    state_shape = jax.ShapeDtypeStruct((8, cols), F32)
    full = pltpu.VMEM((sectors, rows, cols), F32)
    scratch = [pltpu.VMEM((sectors, rows, cols), BF16), full]

    count, entries = left_ops.shape[0], 2 * left_ops.shape[0] + sectors
    ints = [pltpu.SMEM((n,), jnp.int32) for n in (sectors, sectors, count, count, sectors)]
    left, right, table = pl.pallas_call(
        load_kernel,
        out_shape=(
            jax.ShapeDtypeStruct(left_ops.shape, BF16),
            jax.ShapeDtypeStruct(right_ops.shape, BF16),
            jax.ShapeDtypeStruct((entries,), jnp.int32),
        ),
        in_specs=[HBM] * 6,
        out_specs=(VMEM, VMEM, SMEM),
        scratch_shapes=ints + [pltpu.SemaphoreType.DMA((6,))],
        compiler_params=params(),
        cost_estimate=pl.CostEstimate(flops=0, bytes_accessed=4 * left_ops.size, transcendentals=0),
    )(*(pltpu.with_memory_space_constraint(x, pltpu.HBM) for x in (block_rows, owner_map, term_in, term_out, left_ops, right_ops)))

    picked = jnp.where(lax.axis_index("terms") % 2 == 0, trial, precond)
    mine = [picked] + [swap(picked, "sectors", mask) for mask in range(1, lax.axis_size("sectors"))]
    mine, (left, right, table) = lax.optimization_barrier((mine, (left, right, table)))
    other = [swap(x, "terms", 1) for x in mine]
    vec, pre, state, keep, send = pl.pallas_call(
        functools.partial(first_kernel, wire),
        out_shape=(whole, whole, state_shape, part, part),
        in_specs=[VMEM] * (2 * len(mine)) + [SMEM] + [VMEM] * 2,
        out_specs=(VMEM,) * 5,
        scratch_shapes=scratch,
        compiler_params=params(),
    )(*mine, *other, table, left, right)
    for step in range(1, STEPS):
        own = reduce_half(keep, send)
        far = swap(own, "terms", 1)
        vec, state, keep, send = pl.pallas_call(
            functools.partial(middle_kernel, wire, step),
            out_shape=(whole, state_shape, part, part),
            in_specs=[VMEM] * 5 + [SMEM] + [VMEM] * 2,
            out_specs=(VMEM,) * 4,
            scratch_shapes=[full] + scratch,
            compiler_params=params(),
        )(own, far, vec, pre, state, table, left, right)
    own = reduce_half(keep, send)
    far = swap(own, "terms", 1)
    vector, energies = pl.pallas_call(
        functools.partial(last_kernel, wire, STEPS),
        out_shape=(jax.ShapeDtypeStruct(trial.shape, F32), state_shape),
        in_specs=[VMEM] * 5 + [SMEM],
        out_specs=(VMEM,) * 2,
        scratch_shapes=[full, full],
        compiler_params=params(),
    )(own, far, vec, pre, state, table)
    return vector, energies[1 : STEPS + 1, 0]


def solution(mesh):
    return jax.shard_map(
        on_device,
        mesh=mesh,
        in_specs=(
            P("sectors", None, None),
            P("sectors", None, None),
            P(),
            P(),
            P(("terms", "sectors")),
            P(("terms", "sectors")),
            P(("terms", "sectors"), None, None),
            P(("terms", "sectors"), None, None),
        ),
        out_specs=(P("sectors", None, None), P()),
        check_vma=False,
    )
```

```python
import functools
import math

import jax
import jax.numpy as jnp
from jax import lax
from jax.experimental import pallas as pl
from jax.experimental.pallas import tpu as pltpu
from jax.sharding import PartitionSpec as P

STEPS = 3
UNROLL = 64
LEFT_MAX = 1.16462404
RIGHT_MAX = 0.010778794
VMEM = pl.BlockSpec(memory_space=pltpu.VMEM)
HBM = pl.BlockSpec(memory_space=pltpu.HBM)
SMEM = pl.BlockSpec(memory_space=pltpu.SMEM)
F32 = jnp.float32
BF16 = jnp.bfloat16
HALF = jnp.float16


def total(tile):
    return jnp.sum(jnp.sum(tile, axis=0, keepdims=True), axis=1, keepdims=True)


def lanes(x):
    rows, cols = x.shape
    return jnp.sum(x.reshape(rows // 8, 8, cols), axis=0)


def live(table, g, acc):
    sectors, rows, cols = acc.shape
    return lax.broadcasted_iota(jnp.int32, (rows, cols), 0) < table[table.shape[0] - sectors + g]


def apply_ops(wire, square, blocks, acc, table, left, right, keep, send):
    sectors, rows, cols = acc.shape
    acc[...] = jnp.zeros_like(acc)
    terms = left.shape[0]
    unroll = math.gcd(UNROLL, terms)

    def group(j, carry):
        for u in range(unroll):
            k = j * unroll + u
            half = jnp.dot(left[k], blocks[table[k]], preferred_element_type=F32)
            acc[table[terms + k]] += jnp.dot(half.astype(BF16), right[k], preferred_element_type=F32)
        return carry

    lax.fori_loop(0, terms // unroll, group, 0)
    gain = (wire / jnp.sqrt(square / (sectors * rows * cols)))[None]
    h = sectors // 2
    low = lax.axis_index("terms") % 2
    keep[...] = acc[pl.ds(low * h, h)] * gain
    send[...] = acc[pl.ds((1 - low) * h, h)] * gain


def load_kernel(rows_hbm, owner_hbm, in_hbm, out_hbm, left_hbm, right_hbm, left, right, table,
                rows_live, owner, term_in, term_out, slot, sems):
    pairs = ((owner_hbm, owner), (in_hbm, term_in), (out_hbm, term_out), (rows_hbm, rows_live),
             (left_hbm, left), (right_hbm, right))
    copies = [pltpu.make_async_copy(src, dst, sems.at[i]) for i, (src, dst) in enumerate(pairs)]
    for copy in copies:
        copy.start()
    for copy in copies[:4]:
        copy.wait()
    sectors, terms = owner.shape[0], term_in.shape[0]
    for i in range(sectors):
        slot[owner[i]] = i
        table[2 * terms + i] = rows_live[i]
    for k in range(terms):
        table[k] = slot[term_in[k]]
        table[terms + k] = slot[term_out[k]]
    for copy in copies[4:]:
        copy.wait()


def place(parts, whole, fill):
    here = lax.axis_index("sectors")
    held = parts[0].shape[0]
    for mask, part in enumerate(parts):
        for i in range(held):
            g = (here ^ mask) * held + i
            whole[g] = fill(g, part[i])


def first_kernel(wire, *refs):
    table, left, right, vec, state, keep, send, blocks, acc = refs[-9:]
    sectors, rows, cols = acc.shape
    place(refs[:-9], vec, lambda g, block: jnp.where(live(table, g, acc), block, 0.0))
    tile = jnp.zeros((8, cols), F32)
    for g in range(sectors):
        v = vec[g]
        blocks[g] = v.astype(BF16)
        tile = tile + lanes(v * v)
    square = jnp.maximum(total(tile), 1e-30)
    state[...] = jnp.broadcast_to(square, state.shape)
    apply_ops(wire, square, blocks, acc, table, left, right, keep, send)


def update(wire, own, far, table, vec, pre, square, full, out):
    sectors, rows, cols = full.shape
    h = sectors // 2
    low = lax.axis_index("terms") % 2
    full[pl.ds(low * h, h)] = own[...]
    full[pl.ds((1 - low) * h, h)] = far[...]
    gain = jnp.sqrt(square / (sectors * rows * cols)) / wire
    tile = jnp.zeros((8, cols), F32)
    for g in range(sectors):
        v = vec[g]
        summed = jnp.where(live(table, g, full), full[g] * gain, 0.0)
        full[g] = summed
        tile = tile + lanes(v * (summed - pre[g] * v))
    rayleigh = total(tile) / square
    tile = jnp.zeros((8, cols), F32)
    for g in range(sectors):
        v = vec[g]
        u = 2.0 * v - (full[g] - rayleigh * v) / pre[g]
        out[g] = u
        tile = tile + lanes(u * u)
    scale = 1.0 / jnp.sqrt(total(tile) / (sectors * rows * cols) + 1e-06)
    return rayleigh, scale


def middle_kernel(wire, step, parts, own, far, vec_in, state_in, table, left, right, *refs):
    vec, state, keep, send, full, blocks, acc = refs[-7:]
    sectors, rows, cols = acc.shape
    pre = refs[0]
    if parts > 1:
        pre = refs[parts]
        place(refs[:parts], pre, lambda g, block: block)
    old = state_in[...]
    rayleigh, scale = update(wire, own, far, table, vec_in, pre, old[0:1, 0:1], full, vec)
    tile = jnp.zeros((8, cols), F32)
    for g in range(sectors):
        v = vec[g] * scale
        vec[g] = v
        blocks[g] = v.astype(BF16)
        tile = tile + lanes(v * v)
    square = jnp.maximum(total(tile), 1e-30)
    line = lax.broadcasted_iota(jnp.int32, old.shape, 0)
    state[...] = jnp.where(line == 0, square, jnp.where(line == step, rayleigh, old))
    apply_ops(wire, square, blocks, acc, table, left, right, keep, send)


def last_kernel(wire, step, own, far, vec_in, state_in, table, pre, out, energies, full, fresh):
    held = out.shape[0]
    old = state_in[...]
    rayleigh, scale = update(wire, own, far, table, vec_in, pre, old[0:1, 0:1], full, fresh)
    first = lax.axis_index("sectors") * held
    out[...] = fresh[pl.ds(first, held)] * scale[None]
    for i in range(1, step):
        energies[i - 1] = jnp.sum(old[i : i + 1, 0:1])
    energies[step - 1] = jnp.sum(rayleigh)


def params():
    return pltpu.CompilerParams(vmem_limit_bytes=24 << 20)


def swap(x, axis, mask):
    return lax.ppermute(x, axis, [(i, i ^ mask) for i in range(lax.axis_size(axis))])


def bit_groups(axis, first):
    count = lax.axis_size(axis).bit_length() - 1
    return [(low, min(2, count - low)) for low in range(first, count, 2)]


def sum_stage(x, axis, low, bits):
    got = [x] + [swap(x, axis, mask << low) for mask in range(1, 1 << bits)]
    got = [g.astype(F32) for g in got]
    while len(got) > 1:
        got = [got[i] + got[i + 1] for i in range(0, len(got), 2)]
    return got[0]


def reduce_half(keep, send):
    x = keep + swap(send, "terms", 1)
    for axis, first in (("terms", 1), ("sectors", 0)):
        for low, bits in bit_groups(axis, first):
            x = sum_stage(lax.optimization_barrier(x.astype(HALF)), axis, low, bits)
    return x


def on_device(trial, precond, block_rows, owner_map, term_in, term_out, left_ops, right_ops):
    sec_local, rows, cols = trial.shape
    sectors = sec_local * lax.axis_size("sectors")
    terms = left_ops.shape[0] * lax.axis_size("sectors") * lax.axis_size("terms")
    bound = 1.02 * LEFT_MAX * RIGHT_MAX * math.sqrt(rows * cols) * math.sqrt(sectors * rows * cols) * terms
    wire = 2.0 ** -max(0, math.ceil(math.log2(bound / 65504.0)))
    whole = jax.ShapeDtypeStruct((sectors, rows, cols), F32)
    part = jax.ShapeDtypeStruct((sectors // 2, rows, cols), F32)
    state_shape = jax.ShapeDtypeStruct((8, cols), F32)
    full = pltpu.VMEM((sectors, rows, cols), F32)
    scratch = [pltpu.VMEM((sectors, rows, cols), BF16), full]

    count, entries = left_ops.shape[0], 2 * left_ops.shape[0] + sectors
    ints = [pltpu.SMEM((n,), jnp.int32) for n in (sectors, sectors, count, count, sectors)]
    left, right, table = pl.pallas_call(
        load_kernel,
        out_shape=(
            jax.ShapeDtypeStruct(left_ops.shape, BF16),
            jax.ShapeDtypeStruct(right_ops.shape, BF16),
            jax.ShapeDtypeStruct((entries,), jnp.int32),
        ),
        in_specs=[HBM] * 6,
        out_specs=(VMEM, VMEM, SMEM),
        scratch_shapes=ints + [pltpu.SemaphoreType.DMA((6,))],
        compiler_params=params(),
        cost_estimate=pl.CostEstimate(flops=0, bytes_accessed=4 * left_ops.size, transcendentals=0),
    )(*(pltpu.with_memory_space_constraint(x, pltpu.HBM) for x in (block_rows, owner_map, term_in, term_out, left_ops, right_ops)))

    masks = range(1, lax.axis_size("sectors"))
    mine = [trial] + [swap(trial, "sectors", mask) for mask in masks]
    precond, left, right, table = lax.optimization_barrier((precond, left, right, table))
    pre = [precond] + [swap(precond, "sectors", mask) for mask in masks]
    mine, (left, right, table) = lax.optimization_barrier((mine, (left, right, table)))
    vec, state, keep, send = pl.pallas_call(
        functools.partial(first_kernel, wire),
        out_shape=(whole, state_shape, part, part),
        in_specs=[VMEM] * len(mine) + [SMEM] + [VMEM] * 2,
        out_specs=(VMEM,) * 4,
        scratch_shapes=scratch,
        compiler_params=params(),
    )(*mine, table, left, right)
    pre, (keep, send) = lax.optimization_barrier((pre, (keep, send)))
    for step in range(1, STEPS):
        own = reduce_half(keep, send)
        far = swap(own, "terms", 1)
        placed = [whole] if len(pre) > 1 else []
        got = pl.pallas_call(
            functools.partial(middle_kernel, wire, step, len(pre)),
            out_shape=(*placed, whole, state_shape, part, part),
            in_specs=[VMEM] * 4 + [SMEM] + [VMEM] * (2 + len(pre)),
            out_specs=(VMEM,) * (4 + len(placed)),
            scratch_shapes=[full] + scratch,
            compiler_params=params(),
        )(own, far, vec, state, table, left, right, *pre)
        pre = [got[0]] if placed else pre
        vec, state, keep, send = got[-4:]
    own = reduce_half(keep, send)
    far = swap(own, "terms", 1)
    return pl.pallas_call(
        functools.partial(last_kernel, wire, STEPS),
        out_shape=(jax.ShapeDtypeStruct(trial.shape, F32), jax.ShapeDtypeStruct((STEPS,), F32)),
        in_specs=[VMEM] * 4 + [SMEM] + [VMEM] * len(pre),
        out_specs=(VMEM, SMEM),
        scratch_shapes=[full, full],
        compiler_params=params(),
    )(own, far, vec, state, table, *pre)


def solution(mesh):
    return jax.shard_map(
        on_device,
        mesh=mesh,
        in_specs=(
            P("sectors", None, None),
            P("sectors", None, None),
            P(),
            P(),
            P(("terms", "sectors")),
            P(("terms", "sectors")),
            P(("terms", "sectors"), None, None),
            P(("terms", "sectors"), None, None),
        ),
        out_specs=(P("sectors", None, None), P()),
        check_vma=False,
    )
```

```python
import functools
import math

import jax
import jax.numpy as jnp
from jax import lax
from jax.experimental import pallas as pl
from jax.experimental.pallas import tpu as pltpu
from jax.sharding import PartitionSpec as P

STEPS = 3
UNROLL = 64
LEFT_MAX = 1.16462404
RIGHT_MAX = 0.010778794
VMEM = pl.BlockSpec(memory_space=pltpu.VMEM)
HBM = pl.BlockSpec(memory_space=pltpu.HBM)
SMEM = pl.BlockSpec(memory_space=pltpu.SMEM)
F32 = jnp.float32
BF16 = jnp.bfloat16
HALF = jnp.float16


def total(tile):
    return jnp.sum(jnp.sum(tile, axis=0, keepdims=True), axis=1, keepdims=True)


def lanes(x):
    rows, cols = x.shape
    return jnp.sum(x.reshape(rows // 8, 8, cols), axis=0)


def live(table, g, acc):
    sectors, rows, cols = acc.shape
    return lax.broadcasted_iota(jnp.int32, (rows, cols), 0) < table[table.shape[0] - sectors + g]


def apply_ops(wire, square, blocks, acc, table, left, right, keep, send):
    sectors, rows, cols = acc.shape
    acc[...] = jnp.zeros_like(acc)
    terms = left.shape[0]
    unroll = math.gcd(UNROLL, terms)

    def group(j, carry):
        for u in range(unroll):
            k = j * unroll + u
            half = jnp.dot(left[k], blocks[table[k]], preferred_element_type=F32)
            acc[table[terms + k]] += jnp.dot(half.astype(BF16), right[k], preferred_element_type=F32)
        return carry

    lax.fori_loop(0, terms // unroll, group, 0)
    gain = (wire / jnp.sqrt(square / (sectors * rows * cols)))[None]
    h = sectors // 2
    low = lax.axis_index("terms") % 2
    keep[...] = acc[pl.ds(low * h, h)] * gain
    send[...] = acc[pl.ds((1 - low) * h, h)] * gain


def load_kernel(rows_hbm, owner_hbm, in_hbm, out_hbm, left_hbm, right_hbm, left, right, table,
                rows_live, owner, term_in, term_out, slot, sems):
    pairs = ((owner_hbm, owner), (in_hbm, term_in), (out_hbm, term_out), (rows_hbm, rows_live),
             (left_hbm, left), (right_hbm, right))
    copies = [pltpu.make_async_copy(src, dst, sems.at[i]) for i, (src, dst) in enumerate(pairs)]
    for copy in copies:
        copy.start()
    for copy in copies[:4]:
        copy.wait()
    sectors, terms = owner.shape[0], term_in.shape[0]
    for i in range(sectors):
        slot[owner[i]] = i
        table[2 * terms + i] = rows_live[i]
    for k in range(terms):
        table[k] = slot[term_in[k]]
        table[terms + k] = slot[term_out[k]]
    for copy in copies[4:]:
        copy.wait()


def place(parts, whole, fill):
    here = lax.axis_index("sectors")
    held = parts[0].shape[0]
    for mask, part in enumerate(parts):
        for i in range(held):
            g = (here ^ mask) * held + i
            whole[g] = fill(g, part[i])


def first_kernel(wire, *refs):
    table, left, right, vec, pre, state, keep, send, blocks, acc = refs[-10:]
    sectors, rows, cols = acc.shape
    parts = (len(refs) - 10) // 2
    mine, other = refs[:parts], refs[parts : 2 * parts]
    low = lax.axis_index("terms") % 2

    def load(trial, precond):
        place(trial, vec, lambda g, block: jnp.where(live(table, g, acc), block, 0.0))
        place(precond, pre, lambda g, block: block)

    @pl.when(low == 0)
    def _():
        load(mine, other)

    @pl.when(low == 1)
    def _():
        load(other, mine)

    tile = jnp.zeros((8, cols), F32)
    for g in range(sectors):
        v = vec[g]
        blocks[g] = v.astype(BF16)
        tile = tile + lanes(v * v)
    square = jnp.maximum(total(tile), 1e-30)
    state[...] = jnp.broadcast_to(square, state.shape)
    apply_ops(wire, square, blocks, acc, table, left, right, keep, send)


def update(wire, own, far, table, vec, pre, square, full, out):
    sectors, rows, cols = full.shape
    h = sectors // 2
    low = lax.axis_index("terms") % 2
    full[pl.ds(low * h, h)] = own[...]
    full[pl.ds((1 - low) * h, h)] = far[...]
    gain = jnp.sqrt(square / (sectors * rows * cols)) / wire
    tile = jnp.zeros((8, cols), F32)
    for g in range(sectors):
        v = vec[g]
        summed = jnp.where(live(table, g, full), full[g] * gain, 0.0)
        full[g] = summed
        tile = tile + lanes(v * (summed - pre[g] * v))
    rayleigh = total(tile) / square
    tile = jnp.zeros((8, cols), F32)
    for g in range(sectors):
        v = vec[g]
        u = 2.0 * v - (full[g] - rayleigh * v) / pre[g]
        out[g] = u
        tile = tile + lanes(u * u)
    scale = 1.0 / jnp.sqrt(total(tile) / (sectors * rows * cols) + 1e-06)
    return rayleigh, scale


def middle_kernel(wire, step, own, far, vec_in, pre, state_in, table, left, right,
                  vec, state, keep, send, full, blocks, acc):
    sectors, rows, cols = acc.shape
    old = state_in[...]
    rayleigh, scale = update(wire, own, far, table, vec_in, pre, old[0:1, 0:1], full, vec)
    tile = jnp.zeros((8, cols), F32)
    for g in range(sectors):
        v = vec[g] * scale
        vec[g] = v
        blocks[g] = v.astype(BF16)
        tile = tile + lanes(v * v)
    square = jnp.maximum(total(tile), 1e-30)
    line = lax.broadcasted_iota(jnp.int32, old.shape, 0)
    state[...] = jnp.where(line == 0, square, jnp.where(line == step, rayleigh, old))
    apply_ops(wire, square, blocks, acc, table, left, right, keep, send)


def last_kernel(wire, step, own, far, vec_in, pre, state_in, table, out, energies, full, fresh):
    held = out.shape[0]
    old = state_in[...]
    rayleigh, scale = update(wire, own, far, table, vec_in, pre, old[0:1, 0:1], full, fresh)
    first = lax.axis_index("sectors") * held
    out[...] = fresh[pl.ds(first, held)] * scale[None]
    for i in range(1, step):
        energies[i - 1] = jnp.sum(old[i : i + 1, 0:1])
    energies[step - 1] = jnp.sum(rayleigh)


def params():
    return pltpu.CompilerParams(vmem_limit_bytes=24 << 20)


def swap(x, axis, mask):
    return lax.ppermute(x, axis, [(i, i ^ mask) for i in range(lax.axis_size(axis))])


def stages(axis, first):
    count = lax.axis_size(axis).bit_length() - 1
    one = 1 if axis == "sectors" else lax.axis_size("sectors")
    return [[mask * one << low for mask in range(1, 1 << min(2, count - low))] for low in range(first, count, 2)]


def exchange(x, masks):
    sectors = lax.axis_size("sectors")
    devices = range(sectors * lax.axis_size("terms"))
    return lax.ppermute(x, ("terms", "sectors"), [(d, d ^ masks[d // sectors % 2]) for d in devices])


def reduce_half(keep, send):
    x = keep + swap(send, "terms", 1)
    along, across = stages("terms", 1), stages("sectors", 0)
    orders = along + across, across + along
    if [len(s) for s in orders[0]] != [len(s) for s in orders[1]]:
        orders = orders[0], orders[0]
    for even, odd in zip(*orders):
        x = lax.optimization_barrier(x.astype(HALF))
        got = [x] + [exchange(x, masks) for masks in zip(even, odd)]
        got = [g.astype(F32) for g in got]
        while len(got) > 1:
            got = [got[i] + got[i + 1] for i in range(0, len(got), 2)]
        x = got[0]
    return x


def on_device(trial, precond, block_rows, owner_map, term_in, term_out, left_ops, right_ops):
    sec_local, rows, cols = trial.shape
    sectors = sec_local * lax.axis_size("sectors")
    terms = left_ops.shape[0] * lax.axis_size("sectors") * lax.axis_size("terms")
    bound = 1.02 * LEFT_MAX * RIGHT_MAX * math.sqrt(rows * cols) * math.sqrt(sectors * rows * cols) * terms
    wire = 2.0 ** -max(0, math.ceil(math.log2(bound / 65504.0)))
    whole = jax.ShapeDtypeStruct((sectors, rows, cols), F32)
    part = jax.ShapeDtypeStruct((sectors // 2, rows, cols), F32)
    state_shape = jax.ShapeDtypeStruct((8, cols), F32)
    full = pltpu.VMEM((sectors, rows, cols), F32)
    scratch = [pltpu.VMEM((sectors, rows, cols), BF16), full]

    count, entries = left_ops.shape[0], 2 * left_ops.shape[0] + sectors
    ints = [pltpu.SMEM((n,), jnp.int32) for n in (sectors, sectors, count, count, sectors)]
    left, right, table = pl.pallas_call(
        load_kernel,
        out_shape=(
            jax.ShapeDtypeStruct(left_ops.shape, BF16),
            jax.ShapeDtypeStruct(right_ops.shape, BF16),
            jax.ShapeDtypeStruct((entries,), jnp.int32),
        ),
        in_specs=[HBM] * 6,
        out_specs=(VMEM, VMEM, SMEM),
        scratch_shapes=ints + [pltpu.SemaphoreType.DMA((6,))],
        compiler_params=params(),
        cost_estimate=pl.CostEstimate(flops=0, bytes_accessed=4 * left_ops.size, transcendentals=0),
    )(*(pltpu.with_memory_space_constraint(x, pltpu.HBM) for x in (block_rows, owner_map, term_in, term_out, left_ops, right_ops)))

    picked = jnp.where(lax.axis_index("terms") % 2 == 0, trial, precond)
    swapped = swap(picked, "terms", 1)
    mine = [swap(picked, "sectors", mask) for mask in range(1, lax.axis_size("sectors"))]
    mine, (left, right, table) = lax.optimization_barrier((mine, (left, right, table)))
    other = [swapped] + [swap(x, "terms", 1) for x in mine]
    mine = [picked] + mine
    vec, pre, state, keep, send = pl.pallas_call(
        functools.partial(first_kernel, wire),
        out_shape=(whole, whole, state_shape, part, part),
        in_specs=[VMEM] * (2 * len(mine)) + [SMEM] + [VMEM] * 2,
        out_specs=(VMEM,) * 5,
        scratch_shapes=scratch,
        compiler_params=params(),
    )(*mine, *other, table, left, right)
    for step in range(1, STEPS):
        own = reduce_half(keep, send)
        far = swap(own, "terms", 1)
        vec, state, keep, send = pl.pallas_call(
            functools.partial(middle_kernel, wire, step),
            out_shape=(whole, state_shape, part, part),
            in_specs=[VMEM] * 5 + [SMEM] + [VMEM] * 2,
            out_specs=(VMEM,) * 4,
            scratch_shapes=[full] + scratch,
            compiler_params=params(),
        )(own, far, vec, pre, state, table, left, right)
    own = reduce_half(keep, send)
    far = swap(own, "terms", 1)
    return pl.pallas_call(
        functools.partial(last_kernel, wire, STEPS),
        out_shape=(jax.ShapeDtypeStruct(trial.shape, F32), jax.ShapeDtypeStruct((STEPS,), F32)),
        in_specs=[VMEM] * 5 + [SMEM],
        out_specs=(VMEM, SMEM),
        scratch_shapes=[full, full],
        compiler_params=params(),
    )(own, far, vec, pre, state, table)


def solution(mesh):
    return jax.shard_map(
        on_device,
        mesh=mesh,
        in_specs=(
            P("sectors", None, None),
            P("sectors", None, None),
            P(),
            P(),
            P(("terms", "sectors")),
            P(("terms", "sectors")),
            P(("terms", "sectors"), None, None),
            P(("terms", "sectors"), None, None),
        ),
        out_specs=(P("sectors", None, None), P()),
        check_vma=False,
    )
```

```python
import functools
import math

import jax
import jax.numpy as jnp
from jax import lax
from jax.experimental import pallas as pl
from jax.experimental.pallas import tpu as pltpu
from jax.sharding import PartitionSpec as P

STEPS = 3
UNROLL = 64
LEFT_MAX = 1.16462404
RIGHT_MAX = 0.010778794
VMEM = pl.BlockSpec(memory_space=pltpu.VMEM)
ANY = pl.BlockSpec(memory_space=pl.ANY)
HBM = pl.BlockSpec(memory_space=pltpu.HBM)
SMEM = pl.BlockSpec(memory_space=pltpu.SMEM)
F32 = jnp.float32
BF16 = jnp.bfloat16
HALF = jnp.float16


def total(tile):
    return jnp.sum(jnp.sum(tile, axis=0, keepdims=True), axis=1, keepdims=True)


def lanes(x):
    rows, cols = x.shape
    return jnp.sum(x.reshape(rows // 8, 8, cols), axis=0)


def live(table, g, acc):
    sectors, rows, cols = acc.shape
    return lax.broadcasted_iota(jnp.int32, (rows, cols), 0) < table[table.shape[0] - sectors + g]


def halves(sectors):
    h = sectors // 2
    low = lax.axis_index("terms") % 2
    return low * h, (1 - low) * h


def apply_ops(wire, square, blocks, acc, table, left, right, keep, send):
    sectors, rows, cols = acc.shape
    acc[...] = jnp.zeros_like(acc)
    terms = left.shape[0]
    unroll = math.gcd(UNROLL, terms)

    def group(j, carry):
        for u in range(unroll):
            k = j * unroll + u
            half = jnp.dot(left[k], blocks[table[k]], preferred_element_type=F32)
            acc[table[terms + k]] += jnp.dot(half.astype(BF16), right[k], preferred_element_type=F32)
        return carry

    lax.fori_loop(0, terms // unroll, group, 0)
    gain = (wire / jnp.sqrt(square / (sectors * rows * cols)))[None]
    own, far = halves(sectors)
    keep[...] = acc[pl.ds(own, sectors // 2)] * gain
    send[...] = acc[pl.ds(far, sectors // 2)] * gain


def note(state, old, values):
    line = lax.broadcasted_iota(jnp.int32, state.shape, 0)
    tile = old
    for row, value in values:
        tile = jnp.where(line == row, value, tile)
    state[...] = tile


def load_kernel(rows_hbm, owner_hbm, in_hbm, out_hbm, left_hbm, right_hbm, left, right, table,
                rows_live, owner, term_in, term_out, slot, sems):
    pairs = ((owner_hbm, owner), (in_hbm, term_in), (out_hbm, term_out), (rows_hbm, rows_live),
             (left_hbm, left), (right_hbm, right))
    copies = [pltpu.make_async_copy(src, dst, sems.at[i]) for i, (src, dst) in enumerate(pairs)]
    for copy in copies:
        copy.start()
    for copy in copies[:4]:
        copy.wait()
    sectors, terms = owner.shape[0], term_in.shape[0]
    for i in range(sectors):
        slot[owner[i]] = i
        table[2 * terms + i] = rows_live[i]
    for k in range(terms):
        table[k] = slot[term_in[k]]
        table[terms + k] = slot[term_out[k]]
    for copy in copies[4:]:
        copy.wait()


def place(parts, whole, fill):
    here = lax.axis_index("sectors")
    held = parts[0].shape[0]
    for mask, part in enumerate(parts):
        for i in range(held):
            g = (here ^ mask) * held + i
            whole[g] = fill(g, part[i])


def first_kernel(wire, *refs):
    table, left, right, vec, pre, inv, state, keep, send, blocks, acc = refs[-11:]
    sectors, rows, cols = acc.shape
    parts = (len(refs) - 11) // 2
    mine, other = refs[:parts], refs[parts : 2 * parts]
    low = lax.axis_index("terms") % 2

    def load(trial, precond):
        place(trial, vec, lambda g, block: jnp.where(live(table, g, acc), block, 0.0))
        place(precond, pre, lambda g, block: block)

    @pl.when(low == 0)
    def _():
        load(mine, other)

    @pl.when(low == 1)
    def _():
        load(other, mine)

    squares = weighted = jnp.zeros((8, cols), F32)
    for g in range(sectors):
        v = vec[g]
        blocks[g] = v.astype(BF16)
        inv[g] = jnp.where(live(table, g, acc), 1.0 / pre[g], 0.0)
        squares = squares + lanes(v * v)
        weighted = weighted + lanes(pre[g] * (v * v))
    square = jnp.maximum(total(squares), 1e-30)
    note(state, jnp.zeros(state.shape, F32), ((0, square), (1, total(weighted))))
    apply_ops(wire, square, blocks, acc, table, left, right, keep, send)


def update(wire, sums, vec, inv, old, out):
    sectors, rows, cols = out.shape
    zero = jnp.zeros((8, cols), F32)
    square, weighted = old[0:1, 0:1], old[1:2, 0:1]
    gain = jnp.sqrt(square / (sectors * rows * cols)) / wire
    tiles = []
    for base, part in zip(halves(sectors), sums):
        tile = zero
        for j in range(sectors // 2):
            tile = tile + lanes(vec[base + j] * part[j])
        tiles.append(tile)
    rayleigh = (total(tiles[0] + tiles[1]) * gain - weighted) / square
    tiles = []
    for base, part in zip(halves(sectors), sums):
        tile = zero
        for j in range(sectors // 2):
            v = vec[base + j]
            u = 2.0 * v - (part[j] * gain - rayleigh * v) * inv[base + j]
            out[base + j] = u
            tile = tile + lanes(u * u)
        tiles.append(tile)
    scale = 1.0 / jnp.sqrt(total(tiles[0] + tiles[1]) / (sectors * rows * cols) + 1e-06)
    return rayleigh, scale


def middle_kernel(wire, step, own, far, vec_in, pre, inv, state_in, table_in, left, right,
                  vec, state, keep, send, blocks, acc, table, sem):
    sectors, rows, cols = acc.shape
    copy = pltpu.make_async_copy(table_in, table, sem)
    copy.start()
    old = state_in[...]
    rayleigh, scale = update(wire, (own, far), vec_in, inv, old, vec)
    squares = weighted = jnp.zeros((8, cols), F32)
    for g in range(sectors):
        v = vec[g] * scale
        vec[g] = v
        blocks[g] = v.astype(BF16)
        squares = squares + lanes(v * v)
        weighted = weighted + lanes(pre[g] * (v * v))
    square = jnp.maximum(total(squares), 1e-30)
    note(state, old, ((0, square), (1, total(weighted)), (1 + step, rayleigh)))
    copy.wait()
    apply_ops(wire, square, blocks, acc, table, left, right, keep, send)


def last_kernel(wire, step, own, far, vec, inv, state, out, energies, fresh):
    held = out.shape[0]
    old = state[...]
    rayleigh, scale = update(wire, (own, far), vec, inv, old, fresh)
    first = lax.axis_index("sectors") * held
    out[...] = fresh[pl.ds(first, held)] * scale[None]
    for i in range(1, step):
        energies[i - 1] = jnp.sum(old[i + 1 : i + 2, 0:1])
    energies[step - 1] = jnp.sum(rayleigh)


def params():
    return pltpu.CompilerParams(vmem_limit_bytes=24 << 20)


def swap(x, axis, mask):
    return lax.ppermute(x, axis, [(i, i ^ mask) for i in range(lax.axis_size(axis))])


def stages(axis, first):
    count = lax.axis_size(axis).bit_length() - 1
    one = 1 if axis == "sectors" else lax.axis_size("sectors")
    return [[mask * one << low for mask in range(1, 1 << min(2, count - low))] for low in range(first, count, 2)]


def exchange(x, masks):
    sectors = lax.axis_size("sectors")
    devices = range(sectors * lax.axis_size("terms"))
    return lax.ppermute(x, ("terms", "sectors"), [(d, d ^ masks[d // sectors % 2]) for d in devices])


def reduce_half(keep, send):
    x = keep + swap(send, "terms", 1)
    along, across = stages("terms", 1), stages("sectors", 0)
    orders = along + across, across + along
    if [len(s) for s in orders[0]] != [len(s) for s in orders[1]]:
        orders = orders[0], orders[0]
    for even, odd in zip(*orders):
        x = lax.optimization_barrier(x.astype(HALF))
        got = [x] + [exchange(x, masks) for masks in zip(even, odd)]
        got = [g.astype(F32) for g in got]
        while len(got) > 1:
            got = [got[i] + got[i + 1] for i in range(0, len(got), 2)]
        x = got[0]
    return x


def on_device(trial, precond, block_rows, owner_map, term_in, term_out, left_ops, right_ops):
    sec_local, rows, cols = trial.shape
    sectors = sec_local * lax.axis_size("sectors")
    terms = left_ops.shape[0] * lax.axis_size("sectors") * lax.axis_size("terms")
    bound = 1.02 * LEFT_MAX * RIGHT_MAX * math.sqrt(rows * cols) * math.sqrt(sectors * rows * cols) * terms
    wire = 2.0 ** -max(0, math.ceil(math.log2(bound / 65504.0)))
    whole = jax.ShapeDtypeStruct((sectors, rows, cols), F32)
    part = jax.ShapeDtypeStruct((sectors // 2, rows, cols), F32)
    state_shape = jax.ShapeDtypeStruct((8, cols), F32)
    full = pltpu.VMEM((sectors, rows, cols), F32)
    scratch = [pltpu.VMEM((sectors, rows, cols), BF16), full]

    count, entries = left_ops.shape[0], 2 * left_ops.shape[0] + sectors
    ints = [pltpu.SMEM((n,), jnp.int32) for n in (sectors, sectors, count, count, sectors)]
    left, right, table = pl.pallas_call(
        load_kernel,
        out_shape=(
            jax.ShapeDtypeStruct(left_ops.shape, BF16),
            jax.ShapeDtypeStruct(right_ops.shape, BF16),
            jax.ShapeDtypeStruct((entries,), jnp.int32),
        ),
        in_specs=[HBM] * 6,
        out_specs=(VMEM, VMEM, SMEM),
        scratch_shapes=ints + [pltpu.SemaphoreType.DMA((6,))],
        compiler_params=params(),
        cost_estimate=pl.CostEstimate(flops=0, bytes_accessed=4 * left_ops.size, transcendentals=0),
    )(*(pltpu.with_memory_space_constraint(x, pltpu.HBM) for x in (block_rows, owner_map, term_in, term_out, left_ops, right_ops)))

    picked = jnp.where(lax.axis_index("terms") % 2 == 0, trial, precond)
    swapped = swap(picked, "terms", 1)
    mine = [swap(picked, "sectors", mask) for mask in range(1, lax.axis_size("sectors"))]
    mine, (left, right, table) = lax.optimization_barrier((mine, (left, right, table)))
    other = [swapped] + [swap(x, "terms", 1) for x in mine]
    mine = [picked] + mine
    vec, pre, inv, state, keep, send = pl.pallas_call(
        functools.partial(first_kernel, wire),
        out_shape=(whole, whole, whole, state_shape, part, part),
        in_specs=[VMEM] * (2 * len(mine)) + [SMEM] + [VMEM] * 2,
        out_specs=(VMEM,) * 6,
        scratch_shapes=scratch,
        compiler_params=params(),
    )(*mine, *other, table, left, right)
    for step in range(1, STEPS):
        own = reduce_half(keep, send)
        far = swap(own, "terms", 1)
        vec, state, keep, send = pl.pallas_call(
            functools.partial(middle_kernel, wire, step),
            out_shape=(whole, state_shape, part, part),
            in_specs=[VMEM] * 6 + [ANY] + [VMEM] * 2,
            out_specs=(VMEM,) * 4,
            scratch_shapes=scratch + [pltpu.SMEM(table.shape, jnp.int32), pltpu.SemaphoreType.DMA],
            compiler_params=params(),
        )(own, far, vec, pre, inv, state, table, left, right)
    own = reduce_half(keep, send)
    far = swap(own, "terms", 1)
    return pl.pallas_call(
        functools.partial(last_kernel, wire, STEPS),
        out_shape=(jax.ShapeDtypeStruct(trial.shape, F32), jax.ShapeDtypeStruct((STEPS,), F32)),
        in_specs=[VMEM] * 5,
        out_specs=(VMEM, SMEM),
        scratch_shapes=[full],
        compiler_params=params(),
    )(own, far, vec, inv, state)


def solution(mesh):
    return jax.shard_map(
        on_device,
        mesh=mesh,
        in_specs=(
            P("sectors", None, None),
            P("sectors", None, None),
            P(),
            P(),
            P(("terms", "sectors")),
            P(("terms", "sectors")),
            P(("terms", "sectors"), None, None),
            P(("terms", "sectors"), None, None),
        ),
        out_specs=(P("sectors", None, None), P()),
        check_vma=False,
    )
```

```python
import functools
import math

import jax
import jax.numpy as jnp
from jax import lax
from jax.experimental import pallas as pl
from jax.experimental.pallas import tpu as pltpu
from jax.sharding import PartitionSpec as P

STEPS = 3
UNROLL = 64
LEFT_MAX = 1.16462404
RIGHT_MAX = 0.010778794
VMEM = pl.BlockSpec(memory_space=pltpu.VMEM)
ANY = pl.BlockSpec(memory_space=pl.ANY)
HBM = pl.BlockSpec(memory_space=pltpu.HBM)
SMEM = pl.BlockSpec(memory_space=pltpu.SMEM)
F32 = jnp.float32
BF16 = jnp.bfloat16
HALF = jnp.float16


def total(tile):
    return jnp.sum(jnp.sum(tile, axis=0, keepdims=True), axis=1, keepdims=True)


def lanes(x):
    rows, cols = x.shape
    return jnp.sum(x.reshape(rows // 8, 8, cols), axis=0)


def live(table, g, acc):
    sectors, rows, cols = acc.shape
    return lax.broadcasted_iota(jnp.int32, (rows, cols), 0) < table[table.shape[0] - sectors + g]


def halves(sectors):
    h = sectors // 2
    low = lax.axis_index("terms") % 2
    return low * h, (1 - low) * h


def apply_ops(wire, square, blocks, acc, table, left, right, keep, send):
    sectors, rows, cols = acc.shape
    acc[...] = jnp.zeros_like(acc)
    terms = left.shape[0]
    unroll = math.gcd(UNROLL, terms)

    def group(j, carry):
        for u in range(unroll):
            k = j * unroll + u
            half = jnp.dot(left[k], blocks[table[k]], preferred_element_type=F32)
            acc[table[terms + k]] += jnp.dot(half.astype(BF16), right[k], preferred_element_type=F32)
        return carry

    lax.fori_loop(0, terms // unroll, group, 0)
    gain = (wire / jnp.sqrt(square / (sectors * rows * cols)))[None]
    own, far = halves(sectors)
    keep[...] = acc[pl.ds(own, sectors // 2)] * gain
    send[...] = acc[pl.ds(far, sectors // 2)] * gain


def note(state, old, values):
    line = lax.broadcasted_iota(jnp.int32, state.shape, 0)
    tile = old
    for row, value in values:
        tile = jnp.where(line == row, value, tile)
    state[...] = tile


def load_kernel(rows_hbm, owner_hbm, in_hbm, out_hbm, left_hbm, right_hbm, left, right, table,
                rows_live, owner, term_in, term_out, slot, sems):
    pairs = ((owner_hbm, owner), (in_hbm, term_in), (out_hbm, term_out), (rows_hbm, rows_live),
             (left_hbm, left), (right_hbm, right))
    copies = [pltpu.make_async_copy(src, dst, sems.at[i]) for i, (src, dst) in enumerate(pairs)]
    for copy in copies:
        copy.start()
    for copy in copies[:4]:
        copy.wait()
    sectors, terms = owner.shape[0], term_in.shape[0]
    for i in range(sectors):
        slot[owner[i]] = i
        table[2 * terms + i] = rows_live[i]
    for k in range(terms):
        table[k] = slot[term_in[k]]
        table[terms + k] = slot[term_out[k]]
    for copy in copies[4:]:
        copy.wait()


def pack_kernel(trial, precond, both, picked, sems):
    held = trial.shape[0]
    copies = [
        pltpu.make_async_copy(src, both.at[pl.ds(i * held, held)], sems.at[i]) for i, src in enumerate((trial, precond))
    ]
    for copy in copies:
        copy.start()
    for copy in copies:
        copy.wait()
    picked[...] = both[pl.ds(lax.axis_index("terms") % 2 * held, held)]


def first_kernel(wire, pairs, last, *refs):
    table, left, right, vec, pre, inv, state, keep, send, blocks, acc = refs[-11:]
    packed, *moved = refs[:-11]
    mine, other = moved[: len(moved) // 2], moved[len(moved) // 2 :]
    sectors, rows, cols = acc.shape
    held = packed.shape[0] // 2
    low = lax.axis_index("terms") % 2
    here = lax.axis_index("sectors")

    def place(mask, i, v, p):
        g = (here ^ mask) * held + i
        vec[g] = jnp.where(live(table, g, acc), v, 0.0)
        pre[g] = p

    for i in range(held):
        place(0, i, packed[i], packed[held + i])
        for (even, odd), near, far in zip(pairs, mine, other):
            place(jnp.where(low == 0, even, odd), i, near[i], near[held + i])
            place(jnp.where(low == 0, odd, even), i, far[i], far[held + i])
        if last:
            near, far = mine[-1][i], other[-1][i]
            place(last, i, jnp.where(low == 0, near, far), jnp.where(low == 0, far, near))

    squares = weighted = jnp.zeros((8, cols), F32)
    for g in range(sectors):
        v = vec[g]
        blocks[g] = v.astype(BF16)
        inv[g] = jnp.where(live(table, g, acc), 1.0 / pre[g], 0.0)
        squares = squares + lanes(v * v)
        weighted = weighted + lanes(pre[g] * (v * v))
    square = jnp.maximum(total(squares), 1e-30)
    note(state, jnp.zeros(state.shape, F32), ((0, square), (1, total(weighted))))
    apply_ops(wire, square, blocks, acc, table, left, right, keep, send)


def update(wire, sums, vec, inv, old, out):
    sectors, rows, cols = out.shape
    zero = jnp.zeros((8, cols), F32)
    square, weighted = old[0:1, 0:1], old[1:2, 0:1]
    gain = jnp.sqrt(square / (sectors * rows * cols)) / wire
    tiles = []
    for base, part in zip(halves(sectors), sums):
        tile = zero
        for j in range(sectors // 2):
            tile = tile + lanes(vec[base + j] * part[j])
        tiles.append(tile)
    rayleigh = (total(tiles[0] + tiles[1]) * gain - weighted) / square
    tiles = []
    for base, part in zip(halves(sectors), sums):
        tile = zero
        for j in range(sectors // 2):
            v = vec[base + j]
            u = 2.0 * v - (part[j] * gain - rayleigh * v) * inv[base + j]
            out[base + j] = u
            tile = tile + lanes(u * u)
        tiles.append(tile)
    scale = 1.0 / jnp.sqrt(total(tiles[0] + tiles[1]) / (sectors * rows * cols) + 1e-06)
    return rayleigh, scale


def middle_kernel(wire, step, own, far, vec_in, pre, inv, state_in, table_in, left, right,
                  vec, state, keep, send, blocks, acc, table, sem):
    sectors, rows, cols = acc.shape
    copy = pltpu.make_async_copy(table_in, table, sem)
    copy.start()
    old = state_in[...]
    rayleigh, scale = update(wire, (own, far), vec_in, inv, old, vec)
    squares = weighted = jnp.zeros((8, cols), F32)
    for g in range(sectors):
        v = vec[g] * scale
        vec[g] = v
        blocks[g] = v.astype(BF16)
        squares = squares + lanes(v * v)
        weighted = weighted + lanes(pre[g] * (v * v))
    square = jnp.maximum(total(squares), 1e-30)
    note(state, old, ((0, square), (1, total(weighted)), (1 + step, rayleigh)))
    copy.wait()
    apply_ops(wire, square, blocks, acc, table, left, right, keep, send)


def last_kernel(wire, step, own, far, vec, inv, state, out, energies, fresh):
    held = out.shape[0]
    old = state[...]
    rayleigh, scale = update(wire, (own, far), vec, inv, old, fresh)
    first = lax.axis_index("sectors") * held
    out[...] = fresh[pl.ds(first, held)] * scale[None]
    for i in range(1, step):
        energies[i - 1] = jnp.sum(old[i + 1 : i + 2, 0:1])
    energies[step - 1] = jnp.sum(rayleigh)


def params():
    return pltpu.CompilerParams(vmem_limit_bytes=24 << 20)


def swap(x, axis, mask):
    return lax.ppermute(x, axis, [(i, i ^ mask) for i in range(lax.axis_size(axis))])


def stages(axis, first):
    count = lax.axis_size(axis).bit_length() - 1
    one = 1 if axis == "sectors" else lax.axis_size("sectors")
    return [[mask * one << low for mask in range(1, 1 << min(2, count - low))] for low in range(first, count, 2)]


def exchange(x, masks):
    sectors = lax.axis_size("sectors")
    devices = range(sectors * lax.axis_size("terms"))
    return lax.ppermute(x, ("terms", "sectors"), [(d, d ^ masks[d // sectors % 2]) for d in devices])


def reduce_half(keep, send):
    x = keep + swap(send, "terms", 1)
    along, across = stages("terms", 1), stages("sectors", 0)
    orders = along + across, across + along
    if [len(s) for s in orders[0]] != [len(s) for s in orders[1]]:
        orders = orders[0], orders[0]
    for even, odd in zip(*orders):
        x = lax.optimization_barrier(x.astype(HALF))
        got = [x] + [exchange(x, masks) for masks in zip(even, odd)]
        got = [g.astype(F32) for g in got]
        while len(got) > 1:
            got = [got[i] + got[i + 1] for i in range(0, len(got), 2)]
        x = got[0]
    return x


def on_device(trial, precond, block_rows, owner_map, term_in, term_out, left_ops, right_ops):
    sec_local, rows, cols = trial.shape
    sectors = sec_local * lax.axis_size("sectors")
    terms = left_ops.shape[0] * lax.axis_size("sectors") * lax.axis_size("terms")
    bound = 1.02 * LEFT_MAX * RIGHT_MAX * math.sqrt(rows * cols) * math.sqrt(sectors * rows * cols) * terms
    wire = 2.0 ** -max(0, math.ceil(math.log2(bound / 65504.0)))
    whole = jax.ShapeDtypeStruct((sectors, rows, cols), F32)
    part = jax.ShapeDtypeStruct((sectors // 2, rows, cols), F32)
    state_shape = jax.ShapeDtypeStruct((8, cols), F32)
    full = pltpu.VMEM((sectors, rows, cols), F32)
    scratch = [pltpu.VMEM((sectors, rows, cols), BF16), full]

    count, entries = left_ops.shape[0], 2 * left_ops.shape[0] + sectors
    ints = [pltpu.SMEM((n,), jnp.int32) for n in (sectors, sectors, count, count, sectors)]
    left, right, table = pl.pallas_call(
        load_kernel,
        out_shape=(
            jax.ShapeDtypeStruct(left_ops.shape, BF16),
            jax.ShapeDtypeStruct(right_ops.shape, BF16),
            jax.ShapeDtypeStruct((entries,), jnp.int32),
        ),
        in_specs=[HBM] * 6,
        out_specs=(VMEM, VMEM, SMEM),
        scratch_shapes=ints + [pltpu.SemaphoreType.DMA((6,))],
        compiler_params=params(),
        cost_estimate=pl.CostEstimate(flops=0, bytes_accessed=4 * left_ops.size, transcendentals=0),
    )(*(pltpu.with_memory_space_constraint(x, pltpu.HBM) for x in (block_rows, owner_map, term_in, term_out, left_ops, right_ops)))

    masks = list(range(1, lax.axis_size("sectors")))
    pairs = [tuple(masks[i : i + 2]) for i in range(0, len(masks) - 1, 2)]
    last = masks[-1] if len(masks) % 2 else 0
    both, picked = pl.pallas_call(
        pack_kernel,
        out_shape=(jax.ShapeDtypeStruct((2 * sec_local, rows, cols), F32), jax.ShapeDtypeStruct(trial.shape, F32)),
        in_specs=[HBM] * 2,
        out_specs=(VMEM,) * 2,
        scratch_shapes=[pltpu.SemaphoreType.DMA((2,))],
        compiler_params=params(),
    )(*(pltpu.with_memory_space_constraint(x, pltpu.HBM) for x in (trial, precond)))
    mine = [exchange(both, pair) for pair in pairs]
    if last:
        mine.append(swap(picked, "sectors", last))
    mine, (left, right, table) = lax.optimization_barrier((mine, (left, right, table)))
    other = [swap(x, "terms", 1) for x in mine]
    vec, pre, inv, state, keep, send = pl.pallas_call(
        functools.partial(first_kernel, wire, pairs, last),
        out_shape=(whole, whole, whole, state_shape, part, part),
        in_specs=[VMEM] * (1 + 2 * len(mine)) + [SMEM] + [VMEM] * 2,
        out_specs=(VMEM,) * 6,
        scratch_shapes=scratch,
        compiler_params=params(),
    )(both, *mine, *other, table, left, right)
    for step in range(1, STEPS):
        own = reduce_half(keep, send)
        far = swap(own, "terms", 1)
        vec, state, keep, send = pl.pallas_call(
            functools.partial(middle_kernel, wire, step),
            out_shape=(whole, state_shape, part, part),
            in_specs=[VMEM] * 6 + [ANY] + [VMEM] * 2,
            out_specs=(VMEM,) * 4,
            scratch_shapes=scratch + [pltpu.SMEM(table.shape, jnp.int32), pltpu.SemaphoreType.DMA],
            compiler_params=params(),
        )(own, far, vec, pre, inv, state, table, left, right)
    own = reduce_half(keep, send)
    far = swap(own, "terms", 1)
    return pl.pallas_call(
        functools.partial(last_kernel, wire, STEPS),
        out_shape=(jax.ShapeDtypeStruct(trial.shape, F32), jax.ShapeDtypeStruct((STEPS,), F32)),
        in_specs=[VMEM] * 5,
        out_specs=(VMEM, SMEM),
        scratch_shapes=[full],
        compiler_params=params(),
    )(own, far, vec, inv, state)


def solution(mesh):
    return jax.shard_map(
        on_device,
        mesh=mesh,
        in_specs=(
            P("sectors", None, None),
            P("sectors", None, None),
            P(),
            P(),
            P(("terms", "sectors")),
            P(("terms", "sectors")),
            P(("terms", "sectors"), None, None),
            P(("terms", "sectors"), None, None),
        ),
        out_specs=(P("sectors", None, None), P()),
        check_vma=False,
    )
```

```python
import functools
import math

import jax
import jax.numpy as jnp
from jax import lax
from jax.experimental import pallas as pl
from jax.experimental.pallas import tpu as pltpu
from jax.sharding import PartitionSpec as P

STEPS = 3
UNROLL = 64
LEFT_MAX = 1.16462404
RIGHT_MAX = 0.010778794
VMEM = pl.BlockSpec(memory_space=pltpu.VMEM)
ANY = pl.BlockSpec(memory_space=pl.ANY)
HBM = pl.BlockSpec(memory_space=pltpu.HBM)
SMEM = pl.BlockSpec(memory_space=pltpu.SMEM)
F32 = jnp.float32
BF16 = jnp.bfloat16
HALF = jnp.float16


def total(tile):
    return jnp.sum(jnp.sum(tile, axis=0, keepdims=True), axis=1, keepdims=True)


def lanes(x):
    rows, cols = x.shape
    return jnp.sum(x.reshape(rows // 8, 8, cols), axis=0)


def live(table, g, acc):
    sectors, rows, cols = acc.shape
    return lax.broadcasted_iota(jnp.int32, (rows, cols), 0) < table[table.shape[0] - sectors + g]


def halves(sectors):
    h = sectors // 2
    low = lax.axis_index("terms") % 2
    return low * h, (1 - low) * h


def apply_ops(wire, square, blocks, acc, table, left, right, keep, send):
    sectors, rows, cols = acc.shape
    acc[...] = jnp.zeros_like(acc)
    terms = left.shape[0]
    unroll = math.gcd(UNROLL, terms)

    def group(j, carry):
        for u in range(unroll):
            k = j * unroll + u
            half = jnp.dot(left[k], blocks[table[k]], preferred_element_type=F32)
            acc[table[terms + k]] += jnp.dot(half.astype(BF16), right[k], preferred_element_type=F32)
        return carry

    lax.fori_loop(0, terms // unroll, group, 0)
    gain = (wire / jnp.sqrt(square / (sectors * rows * cols)))[None]
    own, far = halves(sectors)
    keep[...] = acc[pl.ds(own, sectors // 2)] * gain
    send[...] = acc[pl.ds(far, sectors // 2)] * gain


def note(state, old, values):
    line = lax.broadcasted_iota(jnp.int32, state.shape, 0)
    tile = old
    for row, value in values:
        tile = jnp.where(line == row, value, tile)
    state[...] = tile


def load_kernel(rows_hbm, owner_hbm, in_hbm, out_hbm, left_hbm, right_hbm, left, right, table,
                rows_live, owner, term_in, term_out, slot, sems):
    pairs = ((owner_hbm, owner), (in_hbm, term_in), (out_hbm, term_out), (rows_hbm, rows_live),
             (left_hbm, left), (right_hbm, right))
    copies = [pltpu.make_async_copy(src, dst, sems.at[i]) for i, (src, dst) in enumerate(pairs)]
    for copy in copies:
        copy.start()
    for copy in copies[:4]:
        copy.wait()
    sectors, terms = owner.shape[0], term_in.shape[0]
    for i in range(sectors):
        slot[owner[i]] = i
        table[2 * terms + i] = rows_live[i]
    for k in range(terms):
        table[k] = slot[term_in[k]]
        table[terms + k] = slot[term_out[k]]
    for copy in copies[4:]:
        copy.wait()


def pack_kernel(trial, precond, both, picked, sems):
    held = trial.shape[0]
    copies = [
        pltpu.make_async_copy(src, both.at[pl.ds(i * held, held)], sems.at[i]) for i, src in enumerate((trial, precond))
    ]
    for copy in copies:
        copy.start()
    for copy in copies:
        copy.wait()
    picked[...] = both[pl.ds(lax.axis_index("terms") % 2 * held, held)]


def first_kernel(wire, pairs, last, *refs):
    table, left, right, vec, pre, inv, state, keep, send, blocks, acc = refs[-11:]
    packed, *moved = refs[:-11]
    mine, other = moved[: len(moved) // 2], moved[len(moved) // 2 :]
    sectors, rows, cols = acc.shape
    held = packed.shape[0] // 2
    low = lax.axis_index("terms") % 2
    here = lax.axis_index("sectors")

    def place(mask, i, v, p):
        g = (here ^ mask) * held + i
        vec[g] = jnp.where(live(table, g, acc), v, 0.0)
        pre[g] = p

    for i in range(held):
        place(0, i, packed[i], packed[held + i])
        for (even, odd), near, far in zip(pairs, mine, other):
            place(jnp.where(low == 0, even, odd), i, near[i], near[held + i])
            place(jnp.where(low == 0, odd, even), i, far[i], far[held + i])
        if last:
            near, far = mine[-1][i], other[-1][i]
            place(last, i, jnp.where(low == 0, near, far), jnp.where(low == 0, far, near))

    squares = weighted = jnp.zeros((8, cols), F32)
    for g in range(sectors):
        v = vec[g]
        blocks[g] = v.astype(BF16)
        inv[g] = jnp.where(live(table, g, acc), 1.0 / pre[g], 0.0)
        squares = squares + lanes(v * v)
        weighted = weighted + lanes(pre[g] * (v * v))
    square = jnp.maximum(total(squares), 1e-30)
    note(state, jnp.zeros(state.shape, F32), ((0, square), (1, total(weighted))))
    apply_ops(wire, square, blocks, acc, table, left, right, keep, send)


def update(wire, sums, vec, inv, old, out):
    sectors, rows, cols = out.shape
    zero = jnp.zeros((8, cols), F32)
    square, weighted = old[0:1, 0:1], old[1:2, 0:1]
    gain = jnp.sqrt(square / (sectors * rows * cols)) / wire
    tiles = []
    for base, part in zip(halves(sectors), sums):
        tile = zero
        for j in range(sectors // 2):
            tile = tile + lanes(vec[base + j] * part[j])
        tiles.append(tile)
    rayleigh = (total(tiles[0] + tiles[1]) * gain - weighted) / square
    tiles = []
    for base, part in zip(halves(sectors), sums):
        tile = zero
        for j in range(sectors // 2):
            v = vec[base + j]
            u = 2.0 * v - (part[j] * gain - rayleigh * v) * inv[base + j]
            out[base + j] = u
            tile = tile + lanes(u * u)
        tiles.append(tile)
    scale = 1.0 / jnp.sqrt(total(tiles[0] + tiles[1]) / (sectors * rows * cols) + 1e-06)
    return rayleigh, scale


def middle_kernel(wire, step, own, far, vec_in, pre, inv, state_in, table_in, left, right,
                  vec, state, keep, send, blocks, acc, table, sem):
    sectors, rows, cols = acc.shape
    copy = pltpu.make_async_copy(table_in, table, sem)
    copy.start()
    old = state_in[...]
    rayleigh, scale = update(wire, (own, far), vec_in, inv, old, vec)
    squares = weighted = jnp.zeros((8, cols), F32)
    for g in range(sectors):
        v = vec[g] * scale
        vec[g] = v
        blocks[g] = v.astype(BF16)
        squares = squares + lanes(v * v)
        weighted = weighted + lanes(pre[g] * (v * v))
    square = jnp.maximum(total(squares), 1e-30)
    note(state, old, ((0, square), (1, total(weighted)), (1 + step, rayleigh)))
    copy.wait()
    apply_ops(wire, square, blocks, acc, table, left, right, keep, send)


def last_kernel(wire, step, own, far, vec, inv, state, out, energies, fresh):
    held = out.shape[0]
    old = state[...]
    rayleigh, scale = update(wire, (own, far), vec, inv, old, fresh)
    first = lax.axis_index("sectors") * held
    out[...] = fresh[pl.ds(first, held)] * scale[None]
    for i in range(1, step):
        energies[i - 1] = jnp.sum(old[i + 1 : i + 2, 0:1])
    energies[step - 1] = jnp.sum(rayleigh)


def params():
    return pltpu.CompilerParams(vmem_limit_bytes=24 << 20)


def swap(x, axis, mask):
    return lax.ppermute(x, axis, [(i, i ^ mask) for i in range(lax.axis_size(axis))])


def stages(axis, first):
    count = lax.axis_size(axis).bit_length() - 1
    one = 1 if axis == "sectors" else lax.axis_size("sectors")
    return [[mask * one << low for mask in range(1, 1 << min(2, count - low))] for low in range(first, count, 2)]


def exchange(x, masks):
    sectors = lax.axis_size("sectors")
    devices = range(sectors * lax.axis_size("terms"))
    return lax.ppermute(x, ("terms", "sectors"), [(d, d ^ masks[d // sectors % 2]) for d in devices])


def reduce_half(keep, send):
    x = keep + swap(send, "terms", 1)
    along, across = stages("terms", 1), stages("sectors", 0)
    orders = along + across, across + along
    if [len(s) for s in orders[0]] != [len(s) for s in orders[1]]:
        orders = orders[0], orders[0]
    for even, odd in zip(*orders):
        x = lax.optimization_barrier(x.astype(HALF))
        got = [x] + [exchange(x, masks) for masks in zip(even, odd)]
        got = [g.astype(F32) for g in got]
        while len(got) > 1:
            got = [got[i] + got[i + 1] for i in range(0, len(got), 2)]
        x = got[0]
    return x


def on_device(trial, precond, block_rows, owner_map, term_in, term_out, left_ops, right_ops):
    sec_local, rows, cols = trial.shape
    sectors = sec_local * lax.axis_size("sectors")
    terms = left_ops.shape[0] * lax.axis_size("sectors") * lax.axis_size("terms")
    bound = 1.02 * LEFT_MAX * RIGHT_MAX * math.sqrt(rows * cols) * math.sqrt(sectors * rows * cols) * terms
    wire = 2.0 ** -max(0, math.ceil(math.log2(bound / 65504.0)))
    whole = jax.ShapeDtypeStruct((sectors, rows, cols), F32)
    part = jax.ShapeDtypeStruct((sectors // 2, rows, cols), F32)
    state_shape = jax.ShapeDtypeStruct((8, cols), F32)
    full = pltpu.VMEM((sectors, rows, cols), F32)
    scratch = [pltpu.VMEM((sectors, rows, cols), BF16), full]

    count, entries = left_ops.shape[0], 2 * left_ops.shape[0] + sectors
    ints = [pltpu.SMEM((n,), jnp.int32) for n in (sectors, sectors, count, count, sectors)]
    left, right, table = pl.pallas_call(
        load_kernel,
        out_shape=(
            jax.ShapeDtypeStruct(left_ops.shape, BF16),
            jax.ShapeDtypeStruct(right_ops.shape, BF16),
            jax.ShapeDtypeStruct((entries,), jnp.int32),
        ),
        in_specs=[HBM] * 6,
        out_specs=(VMEM, VMEM, SMEM),
        scratch_shapes=ints + [pltpu.SemaphoreType.DMA((6,))],
        compiler_params=params(),
        cost_estimate=pl.CostEstimate(flops=0, bytes_accessed=4 * left_ops.size, transcendentals=0),
    )(*(pltpu.with_memory_space_constraint(x, pltpu.HBM) for x in (block_rows, owner_map, term_in, term_out, left_ops, right_ops)))

    masks = list(range(1, lax.axis_size("sectors")))
    pairs = [tuple(masks[i : i + 2]) for i in range(0, len(masks) - 1, 2)]
    last = masks[-1] if len(masks) % 2 else 0
    both, picked = pl.pallas_call(
        pack_kernel,
        out_shape=(jax.ShapeDtypeStruct((2 * sec_local, rows, cols), F32), jax.ShapeDtypeStruct(trial.shape, F32)),
        in_specs=[HBM] * 2,
        out_specs=(VMEM,) * 2,
        scratch_shapes=[pltpu.SemaphoreType.DMA((2,))],
        compiler_params=params(),
    )(*(pltpu.with_memory_space_constraint(x, pltpu.HBM) for x in (trial, precond)))
    mine = [exchange(both, pair) for pair in pairs]
    if last:
        mine.append(swap(picked, "sectors", last))
    mine = [lax.optimization_barrier((x, table))[0] for x in mine]
    other = [swap(x, "terms", 1) for x in mine]
    vec, pre, inv, state, keep, send = pl.pallas_call(
        functools.partial(first_kernel, wire, pairs, last),
        out_shape=(whole, whole, whole, state_shape, part, part),
        in_specs=[VMEM] * (1 + 2 * len(mine)) + [SMEM] + [VMEM] * 2,
        out_specs=(VMEM,) * 6,
        scratch_shapes=scratch,
        compiler_params=params(),
    )(both, *mine, *other, table, left, right)
    for step in range(1, STEPS):
        own = reduce_half(keep, send)
        far = swap(own, "terms", 1)
        vec, state, keep, send = pl.pallas_call(
            functools.partial(middle_kernel, wire, step),
            out_shape=(whole, state_shape, part, part),
            in_specs=[VMEM] * 6 + [ANY] + [VMEM] * 2,
            out_specs=(VMEM,) * 4,
            scratch_shapes=scratch + [pltpu.SMEM(table.shape, jnp.int32), pltpu.SemaphoreType.DMA],
            compiler_params=params(),
        )(own, far, vec, pre, inv, state, table, left, right)
    own = reduce_half(keep, send)
    far = swap(own, "terms", 1)
    return pl.pallas_call(
        functools.partial(last_kernel, wire, STEPS),
        out_shape=(jax.ShapeDtypeStruct(trial.shape, F32), jax.ShapeDtypeStruct((STEPS,), F32)),
        in_specs=[VMEM] * 5,
        out_specs=(VMEM, SMEM),
        scratch_shapes=[full],
        compiler_params=params(),
    )(own, far, vec, inv, state)


def solution(mesh):
    return jax.shard_map(
        on_device,
        mesh=mesh,
        in_specs=(
            P("sectors", None, None),
            P("sectors", None, None),
            P(),
            P(),
            P(("terms", "sectors")),
            P(("terms", "sectors")),
            P(("terms", "sectors"), None, None),
            P(("terms", "sectors"), None, None),
        ),
        out_specs=(P("sectors", None, None), P()),
        check_vma=False,
    )
```

```python
import functools
import math

import jax
import jax.numpy as jnp
from jax import lax
from jax.experimental import pallas as pl
from jax.experimental.pallas import tpu as pltpu
from jax.sharding import PartitionSpec as P

STEPS = 3
UNROLL = 64
LEFT_MAX = 1.16462404
RIGHT_MAX = 0.010778794
VMEM = pl.BlockSpec(memory_space=pltpu.VMEM)
ANY = pl.BlockSpec(memory_space=pl.ANY)
HBM = pl.BlockSpec(memory_space=pltpu.HBM)
SMEM = pl.BlockSpec(memory_space=pltpu.SMEM)
F32 = jnp.float32
BF16 = jnp.bfloat16
HALF = jnp.float16


def total(tile):
    return jnp.sum(jnp.sum(tile, axis=0, keepdims=True), axis=1, keepdims=True)


def lanes(x):
    rows, cols = x.shape
    return jnp.sum(x.reshape(rows // 8, 8, cols), axis=0)


def live(table, g, acc):
    sectors, rows, cols = acc.shape
    return lax.broadcasted_iota(jnp.int32, (rows, cols), 0) < table[table.shape[0] - sectors + g]


def halves(sectors):
    h = sectors // 2
    low = lax.axis_index("terms") % 2
    return low * h, (1 - low) * h


def apply_ops(wire, square, blocks, acc, table, left, right, keep, send):
    sectors, rows, cols = acc.shape
    acc[...] = jnp.zeros_like(acc)
    terms = left.shape[0]
    unroll = math.gcd(UNROLL, terms)

    def group(j, carry):
        for u in range(unroll):
            k = j * unroll + u
            half = jnp.dot(left[k], blocks[table[k]], preferred_element_type=F32)
            acc[table[terms + k]] += jnp.dot(half.astype(BF16), right[k], preferred_element_type=F32)
        return carry

    lax.fori_loop(0, terms // unroll, group, 0)
    gain = (wire / jnp.sqrt(square / (sectors * rows * cols)))[None]
    own, far = halves(sectors)
    keep[...] = acc[pl.ds(own, sectors // 2)] * gain
    send[...] = acc[pl.ds(far, sectors // 2)] * gain


def note(state, old, values):
    line = lax.broadcasted_iota(jnp.int32, state.shape, 0)
    tile = old
    for row, value in values:
        tile = jnp.where(line == row, value, tile)
    state[...] = tile


def load_kernel(rows_hbm, owner_hbm, in_hbm, out_hbm, left_hbm, right_hbm, left, right, table,
                rows_live, owner, term_in, term_out, slot, sems):
    pairs = ((owner_hbm, owner), (in_hbm, term_in), (out_hbm, term_out), (rows_hbm, rows_live),
             (left_hbm, left), (right_hbm, right))
    copies = [pltpu.make_async_copy(src, dst, sems.at[i]) for i, (src, dst) in enumerate(pairs)]
    for copy in copies:
        copy.start()
    for copy in copies[:4]:
        copy.wait()
    sectors, terms = owner.shape[0], term_in.shape[0]
    for i in range(sectors):
        slot[owner[i]] = i
        table[2 * terms + i] = rows_live[i]
    for k in range(terms):
        table[k] = slot[term_in[k]]
        table[terms + k] = slot[term_out[k]]
    for copy in copies[4:]:
        copy.wait()


def pack_kernel(trial, precond, both, picked, sems):
    held = trial.shape[0]
    copies = [
        pltpu.make_async_copy(src, both.at[pl.ds(i * held, held)], sems.at[i]) for i, src in enumerate((trial, precond))
    ]
    for copy in copies:
        copy.start()
    for copy in copies:
        copy.wait()
    picked[...] = both[pl.ds(lax.axis_index("terms") % 2 * held, held)]


def first_kernel(wire, pairs, last, *refs):
    table, left, right, vec, pre, inv, state, keep, send, blocks, acc = refs[-11:]
    packed, *moved = refs[:-11]
    mine, other = moved[: len(moved) // 2], moved[len(moved) // 2 :]
    sectors, rows, cols = acc.shape
    held = packed.shape[0] // 2
    low = lax.axis_index("terms") % 2
    here = lax.axis_index("sectors")

    def place(mask, i, v, p):
        g = (here ^ mask) * held + i
        vec[g] = jnp.where(live(table, g, acc), v, 0.0)
        pre[g] = p

    for i in range(held):
        place(0, i, packed[i], packed[held + i])
        for (even, odd), near, far in zip(pairs, mine, other):
            place(jnp.where(low == 0, even, odd), i, near[i], near[held + i])
            place(jnp.where(low == 0, odd, even), i, far[i], far[held + i])
        if last:
            near, far = mine[-1][i], other[-1][i]
            place(last, i, jnp.where(low == 0, near, far), jnp.where(low == 0, far, near))

    squares = weighted = jnp.zeros((8, cols), F32)
    for g in range(sectors):
        v = vec[g]
        blocks[g] = v.astype(BF16)
        inv[g] = jnp.where(live(table, g, acc), 1.0 / pre[g], 0.0)
        squares = squares + lanes(v * v)
        weighted = weighted + lanes(pre[g] * (v * v))
    square = jnp.maximum(total(squares), 1e-30)
    note(state, jnp.zeros(state.shape, F32), ((0, square), (1, total(weighted))))
    apply_ops(wire, square, blocks, acc, table, left, right, keep, send)


def update(wire, sums, vec, inv, old, out):
    sectors, rows, cols = out.shape
    zero = jnp.zeros((8, cols), F32)
    square, weighted = old[0:1, 0:1], old[1:2, 0:1]
    gain = jnp.sqrt(square / (sectors * rows * cols)) / wire
    tiles = []
    for base, part in zip(halves(sectors), sums):
        tile = zero
        for j in range(sectors // 2):
            tile = tile + lanes(vec[base + j] * part[j])
        tiles.append(tile)
    rayleigh = (total(tiles[0] + tiles[1]) * gain - weighted) / square
    tiles = []
    for base, part in zip(halves(sectors), sums):
        tile = zero
        for j in range(sectors // 2):
            v = vec[base + j]
            u = 2.0 * v - (part[j] * gain - rayleigh * v) * inv[base + j]
            out[base + j] = u
            tile = tile + lanes(u * u)
        tiles.append(tile)
    scale = 1.0 / jnp.sqrt(total(tiles[0] + tiles[1]) / (sectors * rows * cols) + 1e-06)
    return rayleigh, scale


def middle_kernel(wire, step, own, far, vec_in, pre, inv, state_in, table_in, left, right,
                  vec, state, keep, send, blocks, acc, table, sem):
    sectors, rows, cols = acc.shape
    copy = pltpu.make_async_copy(table_in, table, sem)
    copy.start()
    old = state_in[...]
    rayleigh, scale = update(wire, (own, far), vec_in, inv, old, vec)
    squares = weighted = jnp.zeros((8, cols), F32)
    for g in range(sectors):
        v = vec[g] * scale
        vec[g] = v
        blocks[g] = v.astype(BF16)
        squares = squares + lanes(v * v)
        weighted = weighted + lanes(pre[g] * (v * v))
    square = jnp.maximum(total(squares), 1e-30)
    note(state, old, ((0, square), (1, total(weighted)), (1 + step, rayleigh)))
    copy.wait()
    apply_ops(wire, square, blocks, acc, table, left, right, keep, send)


def last_kernel(wire, step, own, far, vec, inv, state, out, energies, fresh):
    held = out.shape[0]
    old = state[...]
    rayleigh, scale = update(wire, (own, far), vec, inv, old, fresh)
    first = lax.axis_index("sectors") * held
    out[...] = fresh[pl.ds(first, held)] * scale[None]
    for i in range(1, step):
        energies[i - 1] = jnp.sum(old[i + 1 : i + 2, 0:1])
    energies[step - 1] = jnp.sum(rayleigh)


def params():
    return pltpu.CompilerParams(vmem_limit_bytes=24 << 20)


def swap(x, axis, mask):
    return lax.ppermute(x, axis, [(i, i ^ mask) for i in range(lax.axis_size(axis))])


def stages(axis, first):
    count = lax.axis_size(axis).bit_length() - 1
    one = 1 if axis == "sectors" else lax.axis_size("sectors")
    order = (1, 2, 3) if axis == "sectors" else (1, 3, 2)
    return [[mask * one << low for mask in order[: (1 << min(2, count - low)) - 1]] for low in range(first, count, 2)]


def exchange(x, masks):
    sectors = lax.axis_size("sectors")
    devices = range(sectors * lax.axis_size("terms"))
    return lax.ppermute(x, ("terms", "sectors"), [(d, d ^ masks[d // sectors % 2]) for d in devices])


def reduce_half(keep, send):
    x = keep + swap(send.astype(HALF), "terms", 1).astype(F32)
    along, across = stages("terms", 1), stages("sectors", 0)
    orders = along + across, across + along
    if [len(s) for s in orders[0]] != [len(s) for s in orders[1]]:
        orders = orders[0], orders[0]
    for even, odd in zip(*orders):
        x = lax.optimization_barrier(x.astype(HALF))
        got = [x] + [exchange(x, masks) for masks in zip(even, odd)]
        got = [g.astype(F32) for g in got]
        while len(got) > 1:
            got = [got[i] + got[i + 1] for i in range(0, len(got), 2)]
        x = got[0]
    return x


def on_device(trial, precond, block_rows, owner_map, term_in, term_out, left_ops, right_ops):
    sec_local, rows, cols = trial.shape
    sectors = sec_local * lax.axis_size("sectors")
    terms = left_ops.shape[0] * lax.axis_size("sectors") * lax.axis_size("terms")
    bound = 1.02 * LEFT_MAX * RIGHT_MAX * math.sqrt(rows * cols) * math.sqrt(sectors * rows * cols) * terms
    wire = 2.0 ** -max(0, math.ceil(math.log2(bound / 65504.0)))
    whole = jax.ShapeDtypeStruct((sectors, rows, cols), F32)
    part = jax.ShapeDtypeStruct((sectors // 2, rows, cols), F32)
    state_shape = jax.ShapeDtypeStruct((8, cols), F32)
    full = pltpu.VMEM((sectors, rows, cols), F32)
    scratch = [pltpu.VMEM((sectors, rows, cols), BF16), full]

    count, entries = left_ops.shape[0], 2 * left_ops.shape[0] + sectors
    ints = [pltpu.SMEM((n,), jnp.int32) for n in (sectors, sectors, count, count, sectors)]
    left, right, table = pl.pallas_call(
        load_kernel,
        out_shape=(
            jax.ShapeDtypeStruct(left_ops.shape, BF16),
            jax.ShapeDtypeStruct(right_ops.shape, BF16),
            jax.ShapeDtypeStruct((entries,), jnp.int32),
        ),
        in_specs=[HBM] * 6,
        out_specs=(VMEM, VMEM, SMEM),
        scratch_shapes=ints + [pltpu.SemaphoreType.DMA((6,))],
        compiler_params=params(),
        cost_estimate=pl.CostEstimate(flops=0, bytes_accessed=4 * left_ops.size, transcendentals=0),
    )(*(pltpu.with_memory_space_constraint(x, pltpu.HBM) for x in (block_rows, owner_map, term_in, term_out, left_ops, right_ops)))

    masks = list(range(1, lax.axis_size("sectors")))
    pairs = [tuple(masks[i : i + 2]) for i in range(0, len(masks) - 1, 2)]
    last = masks[-1] if len(masks) % 2 else 0
    both, picked = pl.pallas_call(
        pack_kernel,
        out_shape=(jax.ShapeDtypeStruct((2 * sec_local, rows, cols), F32), jax.ShapeDtypeStruct(trial.shape, F32)),
        in_specs=[HBM] * 2,
        out_specs=(VMEM,) * 2,
        scratch_shapes=[pltpu.SemaphoreType.DMA((2,))],
        compiler_params=params(),
    )(*(pltpu.with_memory_space_constraint(x, pltpu.HBM) for x in (trial, precond)))
    mine = [exchange(both, pair) for pair in pairs]
    if last:
        mine.append(swap(picked, "sectors", last))
    mine = [lax.optimization_barrier((x, table))[0] for x in mine]
    other = [swap(x, "terms", 1) for x in mine]
    vec, pre, inv, state, keep, send = pl.pallas_call(
        functools.partial(first_kernel, wire, pairs, last),
        out_shape=(whole, whole, whole, state_shape, part, part),
        in_specs=[VMEM] * (1 + 2 * len(mine)) + [SMEM] + [VMEM] * 2,
        out_specs=(VMEM,) * 6,
        scratch_shapes=scratch,
        compiler_params=params(),
    )(both, *mine, *other, table, left, right)
    for step in range(1, STEPS):
        own = reduce_half(keep, send)
        far = swap(own, "terms", 1)
        vec, state, keep, send = pl.pallas_call(
            functools.partial(middle_kernel, wire, step),
            out_shape=(whole, state_shape, part, part),
            in_specs=[VMEM] * 6 + [ANY] + [VMEM] * 2,
            out_specs=(VMEM,) * 4,
            scratch_shapes=scratch + [pltpu.SMEM(table.shape, jnp.int32), pltpu.SemaphoreType.DMA],
            compiler_params=params(),
        )(own, far, vec, pre, inv, state, table, left, right)
    own = reduce_half(keep, send)
    far = swap(own, "terms", 1)
    return pl.pallas_call(
        functools.partial(last_kernel, wire, STEPS),
        out_shape=(jax.ShapeDtypeStruct(trial.shape, F32), jax.ShapeDtypeStruct((STEPS,), F32)),
        in_specs=[VMEM] * 5,
        out_specs=(VMEM, SMEM),
        scratch_shapes=[full],
        compiler_params=params(),
    )(own, far, vec, inv, state)


def solution(mesh):
    return jax.shard_map(
        on_device,
        mesh=mesh,
        in_specs=(
            P("sectors", None, None),
            P("sectors", None, None),
            P(),
            P(),
            P(("terms", "sectors")),
            P(("terms", "sectors")),
            P(("terms", "sectors"), None, None),
            P(("terms", "sectors"), None, None),
        ),
        out_specs=(P("sectors", None, None), P()),
        check_vma=False,
    )
```
